256 devices in a mesh: emb: 64 (over z, y, core), seq: 4 (over x).
Axes of the slice: x: 4, y: 4, z: 8, core: 2. Of those that a mesh axis runs over, the one named last changes fastest.
Arguments:
- table: bfloat16 [32768, 256], P('emb'), may hold values from -6 to 6
- owner: int32 [512, 512, 1], P(('emb', 'seq')), may hold values from 0 to 63; in each aligned block of 512 rows (0 to 511, 512 to 1023, ..., all dimensions but the last counted through in order) at most 16 rows name the same one
- row: int32 [512, 512], P(('emb', 'seq')), may hold values from 0 to 511
- conv_weight: float32 [4, 768, 256], replicated, may hold values from -0.21875 to 0.21875
- gain: float32 [4, 256], replicated, may hold values from 0.1 to 1.9
- upstream: bfloat16 [512, 512, 256], P(('emb', 'seq')), may hold values from -6 to 6
Outputs:
- weight_grad: float32 [4, 768, 256], replicated
- gain_grad: float32 [4, 256], replicated
- table_grad: float32 [32768, 256], P('emb')
The draws below stay inside these ranges and needn't reach their ends.
Inputs may be any that keep to these rules, and one draw needn't show every extreme that they name: Within the positions of one micro-batch on one device (aligned blocks of 512 positions, in sequence order), at most 16 have the same owner.
All inputs are finite; a program needn't handle non-finite values.
Results may differ from the reference program's by a relative error of at most 0.022.
Values may be sent and summed in bfloat16 or wider, within the bound.
A program may use at most 64 MiB of HBM per device.

```python
import math
import jax
import jax.numpy as jnp
import numpy as np
from jax import lax

D = 256
KW = 3
LAYERS = 4
L = 512
MB = 2
SEQ_MB = 1
ROWS_DEV = 512
CAP = 16
SEQS = 512
ROWS = 32768
TOKENS = 262144
N_EMB = 64
N_SEQ = 4


def place_ends(values, rng, smallest, high):
    spot = [jax.random.randint(jax.random.fold_in(rng, axis), (), 0, length) for axis, length in enumerate(values.shape)]
    widest = values.shape.index(max(values.shape))
    next_to = spot[:widest] + [(spot[widest] + 1) % values.shape[widest]] + spot[widest + 1:]
    return values.at[tuple(spot)].set(smallest).at[tuple(next_to)].set(high)


def shard_levels(rng, extent, shards, low, high):
    level, own = 1.0, jax.random.fold_in(rng, 6)
    for dim, parts in shards:
        draws = jnp.exp(jax.random.uniform(jax.random.fold_in(own, dim), (parts,), jnp.float32, low / len(shards), high / len(shards)))
        level = level * jnp.repeat(draws, extent[dim] // parts).reshape([-1 if axis == dim else 1 for axis in range(len(extent))])
    return level


def cumulative_ranks(amount, skew):
    loads = [(1 << 20) // math.isqrt(standing ** skew) + 1 for standing in range(1, amount + 1)]
    deviation = 1 + sum(loads) // (1 << 30)
    return np.cumsum(np.array([max(1, weight // deviation) for weight in loads]))


def skewed_ids(own_key, dims, amount, skew):
    grid = cumulative_ranks(amount, skew)
    ticket = jax.random.randint(jax.random.fold_in(own_key, 1), dims, 0, int(grid[amount - 1]))
    rank = jnp.searchsorted(jnp.asarray(grid, jnp.int32), ticket, side="right")
    return jax.random.permutation(jax.random.fold_in(own_key, 2), amount)[rank].astype(jnp.int32)


def shared_out(stream_key, own, number, rows, count, top, bound, skew):
    ranking = jax.random.permutation(stream_key, count)
    crowded, usual = load_shares(count, rows * top, bound, skew, True), load_shares(count, rows * top, bound, skew, False)
    places = jnp.arange(count)

    def named(sizes, offset_by):
        used = int((sizes > 0).sum())
        fixed = max(1, used // 4)
        passed = fixed + (places - fixed + offset_by * (used - fixed)) % max(1, count - fixed)
        return jnp.zeros((count,), jnp.int32).at[ranking[jnp.where(places < fixed, places, passed)]].set(jnp.asarray(sizes, jnp.int32))

    sizes = jnp.where(number % 4 == 0, named(crowded, number // 4), named(usual, number - number // 4 - 1))
    mixed = jax.random.permutation(jax.random.fold_in(own, 3), count)
    giver, sink = mixed[0:count // 2 * 2:2], mixed[1:count // 2 * 2:2]
    slack = jnp.minimum(sizes[giver] - 1, bound - sizes[sink]) // 2
    slack = jnp.where((giver == ranking[0]) | (sink == ranking[0]) | (sizes[sink] == 0), 0, jnp.maximum(slack, 0))
    passed = jax.random.randint(jax.random.fold_in(own, 4), (count // 2,), 0, 1 << 20) % (slack + 1)
    sizes = sizes.at[giver].add(-passed).at[sink].add(passed)
    labels = jnp.searchsorted(jnp.cumsum(sizes), jnp.arange(rows * top), side="right").astype(jnp.int32)
    table = labels.reshape(top, rows).T
    table = table[jax.random.permutation(jax.random.fold_in(own, 1), rows)]
    offset_by = jax.random.randint(jax.random.fold_in(own, 2), (rows, 1), 0, top)
    return jnp.take_along_axis(table, (jnp.arange(top)[None, :] + offset_by) % top, axis=1)


def load_shares(number_of, total, reach, skew, full):
    loads = [(1 << 20) // math.isqrt(standing ** skew) + 1 for standing in range(1, number_of + 1)]
    largest = reach if full else min(reach, max(-(-total // number_of), total * loads[0] // sum(loads)))
    least = 1 if total - largest >= number_of - 1 else 0
    counts, rest = [largest] + [least] * (number_of - 1), total - largest - least * (number_of - 1)
    while rest > 0:
        movable = [i for i in range(1, number_of) if counts[i] < largest] or [i for i in range(1, number_of) if counts[i] < reach]
        mass, budget = sum([loads[i] for i in movable]), rest
        for i in movable:
            more = min(reach - counts[i], max(1, budget * loads[i] // mass), rest)
            counts[i] = counts[i] + more
            rest = rest - more
    return np.array(counts)


def normal_values(key, dims, deviation, reach, cuts=(), held_as=jnp.bfloat16):
    values = jax.random.normal(key, dims, jnp.float32) * deviation
    if len(cuts) > 0:
        values = shard_levels(key, dims, cuts, -0.22, 0.18) * values
    return jnp.clip(values, min=-reach, max=reach).astype(held_as)


def setup_inputs(seed: int = 0) -> dict:
    splits = jax.random.split(jax.random.key(seed), 7)
    table = normal_values(splits[0], (ROWS, D), 1.0, 6.0, ((0, 64),))
    owner_keys = jax.random.split(jax.random.fold_in(splits[1], 1), SEQS * L // (SEQ_MB * L))
    owner_turns = jax.random.permutation(jax.random.fold_in(splits[1], 3), SEQS * L // (SEQ_MB * L))
    owner = jax.vmap(lambda own, number: shared_out(jax.random.fold_in(splits[1], 2), own, number, SEQ_MB * L, N_EMB, 1, CAP, 2))(owner_keys, owner_turns).reshape((SEQS, L, 1))
    row = place_ends(skewed_ids(splits[2], (SEQS, L), ROWS_DEV, 1), jax.random.fold_in(splits[2], 3), 0, ROWS_DEV - 1).astype(jnp.int32)
    conv_weight = normal_values(splits[3], (LAYERS, KW * D, D), (KW * D) ** -0.5, 0.21875, (), jnp.float32)
    gain = jnp.clip(1.0 + 0.18 * jax.random.normal(splits[4], (LAYERS, D), jnp.float32), 0.1, 1.9)
    upstream = normal_values(splits[5], (SEQS, L, D), 1.0, 6.0, ((0, 256),))
    return dict(table=table, owner=owner, row=row, conv_weight=conv_weight, gain=gain, upstream=upstream)


def shift_back(values, steps):
    return jnp.pad(values, ((0, 0), (steps, 0), (0, 0)))[:, :values.shape[1]]

def shift_ahead(values, steps):
    return jnp.pad(values, ((0, 0), (0, steps), (0, 0)))[:, steps:]

def gelu_tanh(values):
    return jax.nn.gelu(values, approximate=True)

def forward_block(state, weight, gain_row, dilation):
    width = state.shape[-1]
    statef = state.astype(jnp.float32)
    centred = statef - lax.optimization_barrier(jnp.mean(statef, axis=-1, keepdims=True))
    inverse = lax.rsqrt(lax.optimization_barrier(jnp.mean(centred * centred, axis=-1, keepdims=True)) + 1e-05)
    normed = centred * inverse
    hidden = (normed * gain_row).astype(jnp.bfloat16)
    stacked = jnp.concatenate([hidden, shift_back(hidden, dilation), shift_back(hidden, 2 * dilation)], axis=-1)
    flat = stacked.reshape(-1, 3 * width)
    conv = jnp.dot(flat, weight.astype(jnp.bfloat16), preferred_element_type=jnp.float32).reshape(state.shape)
    result = (statef + gelu_tanh(conv)).astype(jnp.bfloat16)
    return (result, (flat, normed, inverse, conv))

def backward_block(cotangent, saved, weight, gain_row, dilation):
    flat, normed, inverse, conv = saved
    width = cotangent.shape[-1]
    slope = jax.jvp(gelu_tanh, (conv,), (jnp.ones_like(conv),))[1]
    cotf = cotangent.astype(jnp.float32)
    dconv = (cotf * slope).astype(jnp.bfloat16).reshape(-1, width)
    dweight = lax.dot_general(flat, dconv, (((0,), (0,)), ((), ())), preferred_element_type=jnp.float32)
    dflat = jnp.dot(dconv, weight.astype(jnp.bfloat16).T, preferred_element_type=jnp.float32)
    dflat = dflat.reshape(cotangent.shape[:-1] + (3 * width,))
    dhidden = dflat[..., :width] + shift_ahead(dflat[..., width:2 * width], dilation)
    dhidden = dhidden + shift_ahead(dflat[..., 2 * width:], 2 * dilation)
    dgain = lax.optimization_barrier(jnp.sum(dhidden * normed, axis=(0, 1)))
    dnorm = dhidden * gain_row
    dstate = inverse * (dnorm - lax.optimization_barrier(jnp.mean(dnorm, axis=-1, keepdims=True)) - normed * lax.optimization_barrier(jnp.mean(dnorm * normed, axis=-1, keepdims=True)))
    return ((cotf + dstate).astype(jnp.bfloat16), dweight, dgain)

def run_stack(embed, weights, gains, cotangent):
    state = embed
    saves = []
    for layer in range(weights.shape[0]):
        state, saved = forward_block(state, weights[layer], gains[layer], 2 ** layer)
        saves.append(saved)
    weight_parts = []
    gain_parts = []
    for layer in reversed(range(weights.shape[0])):
        cotangent, dweight, dgain = backward_block(cotangent, saves[layer], weights[layer], gains[layer], 2 ** layer)
        weight_parts.insert(0, dweight)
        gain_parts.insert(0, dgain)
    return (cotangent, jnp.stack(weight_parts), jnp.stack(gain_parts))

def reference(table, owner, row, conv_weight, gain, upstream):
    ids = (owner[:, :, 0] * ROWS_DEV + row).astype(jnp.int32)
    embed = table[ids]
    group = MB * SEQ_MB * N_SEQ
    blocks = SEQS // group

    def one(pair):
        return run_stack(pair[0], conv_weight, gain, pair[1])
    d_embed, weight_parts, gain_parts = lax.map(one, (embed.reshape(blocks, group, L, D), upstream.reshape(blocks, group, L, D)))
    scale = float(TOKENS) ** (-0.5)
    weight_grad = lax.optimization_barrier(jnp.sum(weight_parts, axis=0)) * scale
    gain_grad = lax.optimization_barrier(jnp.sum(gain_parts, axis=0)) * scale
    table_grad = jnp.zeros((ROWS, D), jnp.float32).at[ids.reshape(-1)].add(d_embed.reshape(-1, D).astype(jnp.float32))
    return (weight_grad, gain_grad, table_grad)
```

```python
import functools
import math

import jax
import jax.numpy as jnp
from jax import lax
from jax.experimental import pallas as pl
from jax.experimental.pallas import tpu as pltpu
from jax.sharding import PartitionSpec as P

MB = 2
CAP = 16
LANES = 128
F32 = jnp.float32
BF16 = jnp.bfloat16
I32 = jnp.int32
NT = (((1,), (1,)), ((), ()))
TN = (((0,), (0,)), ((), ()))


def plan(shards, seq_axis):
    core = 2
    y = 4 if shards >= 64 else 2
    return shards // (core * y), y, core, seq_axis


def iota(shape, axis):
    return lax.broadcasted_iota(I32, shape, axis)


def dot(a, b, dims=(((1,), (0,)), ((), ()))):
    return lax.dot_general(a, b, dims, preferred_element_type=F32)


def whole(ref, sem):
    pltpu.make_async_copy(ref, ref, sem).wait()


def greet(peers):
    barrier = pltpu.get_barrier_semaphore()
    total = 0
    for count, device in peers:

        def hello(k, carry, device=device):
            pl.semaphore_signal(barrier, inc=1, device_id=device(k), device_id_type=pl.DeviceIdType.MESH)
            return carry

        lax.fori_loop(0, count, hello, 0)
        total += count
    pl.semaphore_wait(barrier, total)


def scatter_to(count, device, src, dst, send_sem, recv_sem):
    def step(k, carry):
        pltpu.make_async_remote_copy(
            src_ref=src(k),
            dst_ref=dst,
            send_sem=send_sem,
            recv_sem=recv_sem,
            device_id=device(k),
            device_id_type=pl.DeviceIdType.MESH,
        ).start()
        return carry

    lax.fori_loop(0, count, step, 0)


def emb_peer(shards):
    me, x = lax.axis_index("emb"), lax.axis_index("seq")

    def index(k):
        return lax.rem(me + k + 1, shards)

    return index, lambda k: (index(k), x)


def requests(owner, row, shards, lane0):
    tokens = owner.shape[1]
    named = iota((shards, tokens), 0) == owner
    marks = jnp.where(named, 1.0, 0.0).astype(F32)
    upto = jnp.where(iota((tokens, tokens), 0) <= iota((tokens, tokens), 1), 1.0, 0.0).astype(BF16)
    ranks = dot(marks.astype(BF16), upto)
    slot = jnp.sum(marks * ranks, axis=0, keepdims=True).astype(I32) - 1
    high = (row // 16).astype(F32)
    low = (row % 16).astype(F32)
    values = jnp.concatenate([marks * high, marks * low], axis=0).astype(BF16)
    places = jnp.where(iota((LANES, tokens), 0) == slot + lane0, 1.0, 0.0).astype(BF16)
    wanted = dot(values, places, NT)
    wanted = wanted[:shards] * 16.0 + wanted[shards:]
    return owner * CAP + slot, wanted.astype(I32)


def fetch_kernel(shards, seq_axis, owner_ref, row_ref, table_ref, embed_ref, q_ref, ids_ref,
                 ask, asked, serve, fetched, send_sem, recv_sem):
    tokens = row_ref.shape[1]
    rows = table_ref.shape[0]
    me = lax.axis_index("emb")
    index, device = emb_peer(shards)
    groups = shards // 8
    greet([(shards - 1, device)])
    lane0 = lax.rem(me, 8) * CAP
    places = []
    for m in range(MB):
        q, wanted = requests(owner_ref[m : m + 1, :], row_ref[m : m + 1, :], shards, lane0)
        q_ref[m : m + 1, :] = q
        ask[:, m, :] = wanted
        places.append(q)
    mine = pltpu.make_async_copy(ask.at[me], asked.at[me], recv_sem.at[0])
    mine.start()
    scatter_to(shards - 1, device, lambda k: ask.at[index(k)], asked.at[me], send_sem.at[0], recv_sem.at[0])
    whole(asked, recv_sem.at[0])
    for m in range(MB):
        ids = jnp.sum(asked[:, m, :].reshape(groups, 8, LANES), axis=1)
        ids_ref[m] = ids
        tall = jnp.concatenate([ids.astype(F32)] * (LANES // groups), axis=0).T
        for g in range(groups):
            hot = jnp.where(iota((LANES, rows), 1).astype(F32) == tall[:, g : g + 1], 1.0, 0.0).astype(BF16)
            serve[m, g * LANES : (g + 1) * LANES, :] = dot(hot, table_ref[...]).astype(BF16)
        sem = 1 + m
        here = pl.ds(pl.multiple_of(me * CAP, CAP), CAP)
        pltpu.make_async_copy(serve.at[m, here], fetched.at[m, here], recv_sem.at[sem]).start()
        scatter_to(
            shards - 1,
            device,
            lambda k, m=m: serve.at[m, pl.ds(pl.multiple_of(index(k) * CAP, CAP), CAP)],
            fetched.at[m, here],
            send_sem.at[sem],
            recv_sem.at[sem],
        )
    for m in range(MB):
        whole(fetched.at[m], recv_sem.at[1 + m])
        column = jnp.broadcast_to(places[m].astype(F32), (LANES, tokens)).T
        slots = shards * CAP
        hot = jnp.concatenate(
            [
                jnp.where(column == (iota((tokens, LANES), 1) + s).astype(F32), 1.0, 0.0).astype(BF16)
                for s in range(0, slots, LANES)
            ],
            axis=1,
        )
        embed_ref[m] = dot(hot, fetched[m]).astype(BF16)
    whole(ask.at[pl.ds(0, shards - 1)], send_sem.at[0])
    for m in range(MB):
        whole(serve.at[m, pl.ds(0, (shards - 1) * CAP)], send_sem.at[1 + m])


def block_kernel(chunk, embed_ref, weight_ref, gain_ref, up_ref, grad_ref, dweight_ref, dgain_ref,
                 wide, padded, conv, normed, inverse, slope, hidden, dwide):
    layers, taps, width = weight_ref.shape
    tokens = embed_ref.shape[1]
    top = padded.shape[0] - tokens
    pad = top // 2
    for l in range(layers):
        wide[l] = weight_ref[l].astype(BF16)
    padded[0:pad, :] = jnp.zeros((pad, width), F32)
    padded[pad + tokens :, :] = jnp.zeros((pad, width), F32)
    spans = [slice(c, c + chunk) for c in range(0, tokens, chunk)]
    inv_width = 1.0 / width
    k0 = math.sqrt(2.0 / math.pi)
    for m in range(MB):
        for l in range(layers):
            d = 2**l
            if l == 0:
                source = lambda at: embed_ref[m, at, :].astype(F32)
            gain = gain_ref[l : l + 1, :]
            for at in spans:
                if l == 0:
                    state = embed_ref[m, at, :].astype(F32)
                else:
                    state = normed[m, l, at, :]
                centred = state - jnp.sum(state, axis=-1, keepdims=True) * inv_width
                rstd = lax.rsqrt(jnp.sum(centred * centred, axis=-1, keepdims=True) * inv_width + 1e-05)
                norm = centred * rstd
                if l < layers - 1:
                    normed[m, l + 1, at, :] = state
                normed[m, l, at, :] = norm
                inverse[m, l, at, :] = jnp.broadcast_to(rstd, (chunk, LANES))
                padded[pad + at.start : pad + at.stop, :] = norm * gain
            for k in range(3):
                for at in spans:
                    moved = padded[pad + at.start - k * d : pad + at.stop - k * d, :]
                    hidden[m, l, at, k * width : (k + 1) * width] = moved.astype(BF16)
            conv[...] = dot(hidden[m, l], wide[l])
            for at in spans:
                c = conv[at, :]
                c2 = c * c
                t = jnp.tanh(c * (k0 + (k0 * 0.044715) * c2))
                half = 0.5 + 0.5 * t
                slope[m, l, at, :] = half + c * (0.5 - 0.5 * t * t) * (k0 + (3 * k0 * 0.044715) * c2)
                if l < layers - 1:
                    state = normed[m, l + 1, at, :]
                    normed[m, l + 1, at, :] = (state + c * half).astype(BF16).astype(F32)
    for m in range(MB):
        for l in reversed(range(layers)):
            d = 2**l
            gain = gain_ref[l : l + 1, :]
            src = up_ref if l == layers - 1 else grad_ref
            for at in spans:
                padded[pad + at.start : pad + at.stop, :] = src[m, at, :].astype(F32) * slope[m, l, at, :]
            for k in range(3):
                for at in spans:
                    moved = padded[pad + at.start + k * d : pad + at.stop + k * d, :]
                    dwide[m, at, k * width : (k + 1) * width] = moved.astype(BF16)
            for k in range(3):
                part = dot(hidden[m, l, :, 0:width], dwide[m, :, k * width : (k + 1) * width], TN)
                rows = slice(k * width, (k + 1) * width)
                if m == 0:
                    dweight_ref[l, rows, :] = part
                else:
                    dweight_ref[l, rows, :] += part
            dh = dot(dwide[m, :, 0:width], wide[l, 0:width, :], NT)
            dh = dh + dot(dwide[m, :, width : 2 * width], wide[l, width : 2 * width, :], NT)
            dh = dh + dot(dwide[m, :, 2 * width :], wide[l, 2 * width :, :], NT)
            conv[...] = dh
            dgain = jnp.zeros((1, width), F32)
            for at in spans:
                dh = conv[at, :]
                norm = normed[m, l, at, :]
                both = dh * norm
                dgain = dgain + jnp.sum(both, axis=0, keepdims=True)
                dn = dh * gain
                m1 = jnp.sum(dn, axis=-1, keepdims=True) * inv_width
                m2 = jnp.sum(both * gain, axis=-1, keepdims=True) * inv_width
                rstd = inverse[m, l, at, 0:1]
                grad_ref[m, at, :] = (
                    src[m, at, :].astype(F32) + rstd * (dn - m1 - norm * m2)
                ).astype(BF16)
            if m == 0:
                dgain_ref[l : l + 1, :] = dgain
            else:
                dgain_ref[l : l + 1, :] += dgain


def return_kernel(shards, seq_axis, scale, grad_ref, q_ref, ids_ref, dweight_ref, dgain_ref,
                  weight_out, gain_out, table_out,
                  back, returned, tsend, trecv, tall_recv,
                  s0, r0, s1, r1, r2, r3, r4, g0, g1, g2, send_sem, recv_sem, wsend, wrecv):
    z_size, y_size, _, x_size = plan(shards, seq_axis)
    layers, taps, width = dweight_ref.shape
    tokens = grad_ref.shape[1]
    rows = table_out.shape[0]
    slots = shards * CAP
    e, x = lax.axis_index("emb"), lax.axis_index("seq")
    c = lax.rem(e, 2)
    y = lax.rem(e // 2, y_size)
    z = e // (2 * y_size)
    plane = x_size * y_size
    p_me = x * y_size + y
    index, device = emb_peer(shards)
    sibling = (e + 1 - 2 * c, x)

    def x_index(k):
        return lax.rem(x + k + 1, x_size)

    def x_device(k):
        return (e, x_index(k))

    def p_index(k):
        return lax.rem(p_me + k + 1, plane)

    def p_device(k):
        p = p_index(k)
        return ((z * y_size + lax.rem(p, y_size)) * 2 + c, p // y_size)

    def z_device(k):
        return ((lax.rem(z + k + 1, z_size) * y_size + y) * 2 + c, x)

    def off_device(k):
        py = lax.rem(y + 1 + lax.rem(k, y_size - 1), y_size)
        px = lax.rem(x + 1 + k // (y_size - 1), x_size)
        return ((z * y_size + py) * 2 + c, px)

    greet([(shards - 1, device), (x_size - 1, x_device), ((x_size - 1) * (y_size - 1), off_device)])

    here = pl.ds(pl.multiple_of(e * CAP, CAP), CAP)
    for m in range(MB):
        for s in range(0, slots, LANES):
            hot = jnp.where(iota((LANES, tokens), 0) + s == q_ref[m : m + 1, :], 1.0, 0.0).astype(BF16)
            back[m, s : s + LANES, :] = dot(hot, grad_ref[m]).astype(BF16)
        pltpu.make_async_copy(back.at[m, here], returned.at[m, here], recv_sem.at[m]).start()
        scatter_to(
            shards - 1,
            device,
            lambda k, m=m: back.at[m, pl.ds(pl.multiple_of(index(k) * CAP, CAP), CAP)],
            returned.at[m, here],
            send_sem.at[m],
            recv_sem.at[m],
        )

    half = taps // 2
    blocks = plane // 2
    high = half // blocks

    def remote(src, dst, send, recv, to):
        return pltpu.make_async_remote_copy(
            src_ref=src, dst_ref=dst, send_sem=send, recv_sem=recv, device_id=to, device_id_type=pl.DeviceIdType.MESH
        )

    theirs = pl.ds(pl.multiple_of((1 - c) * half, half), half)
    ours = pl.ds(pl.multiple_of(c * half, half), half)
    for l in range(layers):
        s0[l] = dweight_ref[l, theirs, :].astype(BF16)
        remote(s0.at[l], r0.at[l], wsend.at[0, l], wrecv.at[0, l], sibling).start()
    g0[0] = jnp.concatenate([dgain_ref[...], jnp.zeros_like(dgain_ref)], axis=0)
    gain_pair = remote(g0.at[0], g0.at[1], wsend.at[0, layers], wrecv.at[0, layers], sibling)
    gain_pair.start()
    for l in range(layers):
        whole(r0.at[l], wrecv.at[0, l])
        total = dweight_ref[l, ours, :] + r0[l].astype(F32)
        for b in range(blocks):
            for h in range(2):
                s1[l, b * 2 + h] = total[b * high : (b + 1) * high, h * LANES : (h + 1) * LANES].astype(BF16)
        pltpu.make_async_copy(s1.at[l, p_me], r1.at[l, p_me], wrecv.at[1, l]).start()
        scatter_to(plane - 1, p_device, lambda k, l=l: s1.at[l, p_index(k)], r1.at[l, p_me], wsend.at[1, l], wrecv.at[1, l])
    gain_pair.wait_recv()
    g1[p_me] = g0[0] + g0[1]
    scatter_to(plane - 1, p_device, lambda k: g1.at[p_me], g1.at[p_me], wsend.at[1, layers], wrecv.at[1, layers])
    for l in range(layers):
        whole(r1.at[l], wrecv.at[1, l])
        total = jnp.zeros((high, LANES), F32)
        for p in range(plane):
            total = total + r1[l, p].astype(F32)
        r2[l, z] = total.astype(BF16)
        scatter_to(z_size - 1, z_device, lambda k, l=l: r2.at[l, z], r2.at[l, z], wsend.at[2, l], wrecv.at[2, l])
    whole(g1.at[pl.ds(0, plane - 1)], wrecv.at[1, layers])
    whole(g1.at[pl.ds(0, plane - 1)], wsend.at[1, layers])
    total = g1[0]
    for p in range(1, plane):
        total = total + g1[p]
    g2[z] = total
    scatter_to(z_size - 1, z_device, lambda k: g2.at[z], g2.at[z], wsend.at[2, layers], wrecv.at[2, layers])
    for l in range(layers):
        whole(r2.at[l, pl.ds(0, z_size - 1)], wrecv.at[2, l])
        total = r2[l, 0].astype(F32)
        for k in range(1, z_size):
            total = total + r2[l, k].astype(F32)
        r3[l, p_me] = total.astype(BF16)
        scatter_to(plane - 1, p_device, lambda k, l=l: r3.at[l, p_me], r3.at[l, p_me], wsend.at[3, l], wrecv.at[3, l])
    for l in range(layers):
        whole(r3.at[l, pl.ds(0, plane - 1)], wrecv.at[3, l])
        remote(r3.at[l], r4.at[l], wsend.at[4, l], wrecv.at[4, l], sibling).start()

    part = jnp.zeros((rows, width), F32)
    for m in range(MB):
        whole(returned.at[m], recv_sem.at[m])
        hot = jnp.concatenate(
            [
                jnp.where(iota((rows, LANES), 0) == ids_ref[m, g : g + 1, :], 1.0, 0.0).astype(BF16)
                for g in range(slots // LANES)
            ],
            axis=1,
        )
        part = part + dot(hot, returned[m])
    piece = rows // x_size
    tsend[...] = part.astype(BF16).reshape(x_size, piece, width)
    pltpu.make_async_copy(tsend.at[x], trecv.at[x], recv_sem.at[2]).start()
    scatter_to(x_size - 1, x_device, lambda k: tsend.at[x_index(k)], trecv.at[x], send_sem.at[2], recv_sem.at[2])
    whole(trecv, recv_sem.at[2])
    total = trecv[0].astype(F32)
    for k in range(1, x_size):
        total = total + trecv[k].astype(F32)
    tall_recv[x] = total.astype(BF16)
    scatter_to(x_size - 1, x_device, lambda k: tall_recv.at[x], tall_recv.at[x], send_sem.at[3], recv_sem.at[3])

    whole(g2.at[pl.ds(0, z_size - 1)], wrecv.at[2, layers])
    total = g2[0]
    for k in range(1, z_size):
        total = total + g2[k]
    gain_out[...] = total[:layers] * scale
    for l in range(layers):
        whole(r4.at[l], wrecv.at[4, l])
        for b in range(blocks):
            for h in range(2):
                cols = slice(h * LANES, (h + 1) * LANES)
                weight_out[l, pl.ds(pl.multiple_of(c * half + b * high, 8), high), cols] = r3[l, b * 2 + h].astype(F32) * scale
                weight_out[l, pl.ds(pl.multiple_of((1 - c) * half + b * high, 8), high), cols] = (
                    r4[l, b * 2 + h].astype(F32) * scale
                )
    whole(tall_recv.at[pl.ds(0, x_size - 1)], recv_sem.at[3])
    table_out[...] = tall_recv[...].astype(F32).reshape(rows, width)

    for m in range(MB):
        whole(back.at[m, pl.ds(0, slots - CAP)], send_sem.at[m])
    whole(tsend.at[pl.ds(0, x_size - 1)], send_sem.at[2])
    whole(tsend.at[pl.ds(0, x_size - 1)], send_sem.at[3])
    for l in range(layers):
        whole(s0.at[l], wsend.at[0, l])
        whole(s1.at[l, pl.ds(0, plane - 1)], wsend.at[1, l])
        whole(r2.at[l, pl.ds(0, z_size - 1)], wsend.at[2, l])
        whole(r3.at[l, pl.ds(0, plane - 1)], wsend.at[3, l])
        whole(r3.at[l], wsend.at[4, l])
    gain_pair.wait_send()
    whole(g2.at[pl.ds(0, z_size - 1)], wsend.at[2, layers])


def vmem(count):
    return [pl.BlockSpec(memory_space=pltpu.VMEM)] * count


def body(table, owner, row, conv_weight, gain, upstream):
    shards, seq_axis = lax.axis_size("emb"), lax.axis_size("seq")
    _, tokens = row.shape
    rows, width = table.shape
    layers, taps, _ = conv_weight.shape
    slots = shards * CAP
    z_size, y_size, _, x_size = plan(shards, seq_axis)
    plane = x_size * y_size
    limit = 56 * 2**20
    shape = jax.ShapeDtypeStruct
    dma = pltpu.SemaphoreType.DMA
    embed, q, ids = pl.pallas_call(
        functools.partial(fetch_kernel, shards, seq_axis),
        out_shape=[
            shape((MB, tokens, width), BF16),
            shape((MB, tokens), I32),
            shape((MB, shards // 8, LANES), I32),
        ],
        in_specs=vmem(3),
        out_specs=vmem(3),
        scratch_shapes=[
            pltpu.VMEM((shards, MB, LANES), I32),
            pltpu.VMEM((shards, MB, LANES), I32),
            pltpu.VMEM((MB, slots, width), BF16),
            pltpu.VMEM((MB, slots, width), BF16),
            dma((3,)),
            dma((3,)),
        ],
        compiler_params=pltpu.CompilerParams(collective_id=0, has_side_effects=True, vmem_limit_bytes=limit),
    )(owner.reshape(MB, tokens), row, table)
    chunk = 64
    grad, dweight, dgain = pl.pallas_call(
        functools.partial(block_kernel, chunk),
        out_shape=[
            shape((MB, tokens, width), BF16),
            shape((layers, taps, width), F32),
            shape((layers, width), F32),
        ],
        in_specs=vmem(4),
        out_specs=vmem(3),
        scratch_shapes=[
            pltpu.VMEM((layers, taps, width), BF16),
            pltpu.VMEM((tokens + 32, width), F32),
            pltpu.VMEM((tokens, width), F32),
            pltpu.VMEM((MB, layers, tokens, width), F32),
            pltpu.VMEM((MB, layers, tokens, LANES), F32),
            pltpu.VMEM((MB, layers, tokens, width), F32),
            pltpu.VMEM((MB, layers, tokens, taps), BF16),
            pltpu.VMEM((MB, tokens, taps), BF16),
        ],
        compiler_params=pltpu.CompilerParams(vmem_limit_bytes=limit),
    )(embed, conv_weight, gain, upstream)
    half = taps // 2
    high = half // (plane // 2)
    piece = rows // x_size
    scale = float(MB * tokens * shards * seq_axis) ** (-0.5)
    return pl.pallas_call(
        functools.partial(return_kernel, shards, seq_axis, scale),
        out_shape=[
            shape((layers, taps, width), F32),
            shape((layers, width), F32),
            shape((rows, width), F32),
        ],
        in_specs=vmem(5),
        out_specs=vmem(3),
        scratch_shapes=[
            pltpu.VMEM((MB, slots, width), BF16),
            pltpu.VMEM((MB, slots, width), BF16),
            pltpu.VMEM((x_size, piece, width), BF16),
            pltpu.VMEM((x_size, piece, width), BF16),
            pltpu.VMEM((x_size, piece, width), BF16),
            pltpu.VMEM((layers, half, width), BF16),
            pltpu.VMEM((layers, half, width), BF16),
            pltpu.VMEM((layers, plane, high, LANES), BF16),
            pltpu.VMEM((layers, plane, high, LANES), BF16),
            pltpu.VMEM((layers, z_size, high, LANES), BF16),
            pltpu.VMEM((layers, plane, high, LANES), BF16),
            pltpu.VMEM((layers, plane, high, LANES), BF16),
            pltpu.VMEM((2, 2 * layers, width), F32),
            pltpu.VMEM((plane, 2 * layers, width), F32),
            pltpu.VMEM((z_size, 2 * layers, width), F32),
            dma((4,)),
            dma((4,)),
            dma((5, layers + 1)),
            dma((5, layers + 1)),
        ],
        compiler_params=pltpu.CompilerParams(collective_id=1, has_side_effects=True, vmem_limit_bytes=limit),
    )(grad, q, ids, dweight, dgain)


def solution(mesh):
    in_specs = (
        P("emb", None),
        P(("emb", "seq"), None, None),
        P(("emb", "seq"), None),
        P(),
        P(),
        P(("emb", "seq"), None, None),
    )
    out_specs = (P(), P(), P("emb", None))
    return jax.shard_map(body, mesh=mesh, in_specs=in_specs, out_specs=out_specs, check_vma=False)
```

```python
import functools
import math

import jax
import jax.numpy as jnp
from jax import lax
from jax.experimental import pallas as pl
from jax.experimental.pallas import tpu as pltpu
from jax.sharding import PartitionSpec as P

MB = 2
CAP = 16
LANES = 128
F32 = jnp.float32
BF16 = jnp.bfloat16
I32 = jnp.int32
NT = (((1,), (1,)), ((), ()))
TN = (((0,), (0,)), ((), ()))


def plan(shards, seq_axis):
    core = 2
    y = 4 if shards >= 64 else 2
    return shards // (core * y), y, core, seq_axis


def iota(shape, axis):
    return lax.broadcasted_iota(I32, shape, axis)


def dot(a, b, dims=(((1,), (0,)), ((), ()))):
    return lax.dot_general(a, b, dims, preferred_element_type=F32)


def whole(ref, sem):
    pltpu.make_async_copy(ref, ref, sem).wait()


def greet(peers):
    barrier = pltpu.get_barrier_semaphore()
    total = 0
    for count, device in peers:

        def hello(k, carry, device=device):
            pl.semaphore_signal(barrier, inc=1, device_id=device(k), device_id_type=pl.DeviceIdType.MESH)
            return carry

        lax.fori_loop(0, count, hello, 0)
        total += count
    return total


def scatter_to(count, device, src, dst, send_sem, recv_sem):
    def step(k, carry):
        pltpu.make_async_remote_copy(
            src_ref=src(k),
            dst_ref=dst,
            send_sem=send_sem,
            recv_sem=recv_sem,
            device_id=device(k),
            device_id_type=pl.DeviceIdType.MESH,
        ).start()
        return carry

    lax.fori_loop(0, count, step, 0)


def emb_peer(shards):
    me, x = lax.axis_index("emb"), lax.axis_index("seq")

    def index(k):
        return lax.rem(me + k + 1, shards)

    return index, lambda k: (index(k), x)


def requests(owner, row, shards, lane0):
    tokens = owner.shape[1]
    named = iota((shards, tokens), 0) == owner
    marks = jnp.where(named, 1.0, 0.0).astype(F32)
    upto = jnp.where(iota((tokens, tokens), 0) <= iota((tokens, tokens), 1), 1.0, 0.0).astype(BF16)
    ranks = dot(marks.astype(BF16), upto)
    slot = jnp.sum(marks * ranks, axis=0, keepdims=True).astype(I32) - 1
    high = (row // 16).astype(F32)
    low = (row % 16).astype(F32)
    values = jnp.concatenate([marks * high, marks * low], axis=0).astype(BF16)
    places = jnp.where(iota((LANES, tokens), 0) == slot + lane0, 1.0, 0.0).astype(BF16)
    wanted = dot(values, places, NT)
    wanted = wanted[:shards] * 16.0 + wanted[shards:]
    return owner * CAP + slot, wanted.astype(I32)


def window_kernel(shards, seq_axis, chunk,
                  owner_ref, row_ref, table_ref, gain_ref, weight_hbm, up_hbm,
                  weight_out, gain_out, table_out,
                  ask, asked, serve, fetched, back, returned, pick, place, add,
                  weight_ref, up_ref, wide, padded, conv, normed, inverse, slope, hidden, dwide, grad_ref,
                  dweight_ref, tsend, trecv, s0, r0, s1, r1, r2, r3, g0, g1, g2,
                  load_sem, send_sem, recv_sem, wsend, wrecv):
    z_size, y_size, _, x_size = plan(shards, seq_axis)
    layers, taps, width = weight_ref.shape
    tokens = row_ref.shape[1]
    rows = table_ref.shape[0]
    slots = shards * CAP
    groups = shards // 8
    e, x = lax.axis_index("emb"), lax.axis_index("seq")
    c = lax.rem(e, 2)
    y = lax.rem(e // 2, y_size)
    z = e // (2 * y_size)
    plane = x_size * y_size
    p_me = x * y_size + y
    index, device = emb_peer(shards)
    sibling = (e + 1 - 2 * c, x)
    half = taps // 2
    high = half // (plane // 2)
    batches = 2
    deep = layers // batches

    def x_index(k):
        return lax.rem(x + k + 1, x_size)

    def x_device(k):
        return (e, x_index(k))

    def p_index(k):
        return lax.rem(p_me + k + 1, plane)

    def p_device(k):
        p = p_index(k)
        return ((z * y_size + lax.rem(p, y_size)) * 2 + c, p // y_size)

    def z_device(k):
        return ((lax.rem(z + k + 1, z_size) * y_size + y) * 2 + c, x)

    def off_device(k):
        py = lax.rem(y + 1 + lax.rem(k, y_size - 1), y_size)
        px = lax.rem(x + 1 + k // (y_size - 1), x_size)
        return ((z * y_size + py) * 2 + c, px)

    def remote(src, dst, send, recv, to):
        return pltpu.make_async_remote_copy(
            src_ref=src, dst_ref=dst, send_sem=send, recv_sem=recv, device_id=to, device_id_type=pl.DeviceIdType.MESH
        )

    load_weight = pltpu.make_async_copy(weight_hbm, weight_ref, load_sem.at[0])
    load_up = pltpu.make_async_copy(up_hbm, up_ref, load_sem.at[1])
    load_weight.start()
    load_up.start()
    expected = greet([(shards - 1, device), (x_size - 1, x_device), ((x_size - 1) * (y_size - 1), off_device)])

    lane0 = lax.rem(e, 8) * CAP
    places = []
    for m in range(MB):
        q, wanted = requests(owner_ref[m], row_ref[m : m + 1, :], shards, lane0)
        ask[:, m, :] = wanted
        places.append(q)
    pl.semaphore_wait(pltpu.get_barrier_semaphore(), expected)
    pltpu.make_async_copy(ask.at[e], asked.at[e], recv_sem.at[0]).start()
    scatter_to(shards - 1, device, lambda k: ask.at[index(k)], asked.at[e], send_sem.at[0], recv_sem.at[0])

    for m in range(MB):
        column = jnp.broadcast_to(places[m].astype(F32), (LANES, tokens)).T
        for s in range(0, slots, LANES):
            pick[m, :, s : s + LANES] = jnp.where(
                column == (iota((tokens, LANES), 1) + s).astype(F32), 1.0, 0.0
            ).astype(BF16)
            place[m, s : s + LANES, :] = jnp.where(iota((LANES, tokens), 0) + s == places[m], 1.0, 0.0).astype(BF16)
    load_weight.wait()
    for l in range(layers):
        wide[l] = weight_ref[l].astype(BF16)
    pad = (padded.shape[0] - tokens) // 2
    padded[0:pad, :] = jnp.zeros((pad, width), F32)
    padded[pad + tokens :, :] = jnp.zeros((pad, width), F32)

    here = pl.ds(pl.multiple_of(e * CAP, CAP), CAP)
    whole(asked, recv_sem.at[0])
    wanted = []
    for m in range(MB):
        ids = jnp.sum(asked[:, m, :].reshape(groups, 8, LANES), axis=1)
        wanted.append(ids)
        tall = jnp.concatenate([ids.astype(F32)] * (LANES // groups), axis=0).T
        for g in range(groups):
            hot = jnp.where(iota((LANES, rows), 1).astype(F32) == tall[:, g : g + 1], 1.0, 0.0).astype(BF16)
            serve[m, g * LANES : (g + 1) * LANES, :] = dot(hot, table_ref[...]).astype(BF16)
        pltpu.make_async_copy(serve.at[m, here], fetched.at[m, here], recv_sem.at[1 + m]).start()
        scatter_to(
            shards - 1,
            device,
            lambda k, m=m: serve.at[m, pl.ds(pl.multiple_of(index(k) * CAP, CAP), CAP)],
            fetched.at[m, here],
            send_sem.at[1 + m],
            recv_sem.at[1 + m],
        )
    for m in range(MB):
        for g in range(groups):
            add[m, :, g * LANES : (g + 1) * LANES] = jnp.where(
                iota((rows, LANES), 0) == wanted[m][g : g + 1, :], 1.0, 0.0
            ).astype(BF16)
    load_up.wait()

    spans = [slice(at, at + chunk) for at in range(0, tokens, chunk)]
    inv_width = 1.0 / width
    k0 = math.sqrt(2.0 / math.pi)

    def forward(m):
        conv[...] = dot(pick[m], fetched[m])
        for l in range(layers):
            d = 2**l
            gain = gain_ref[l : l + 1, :]
            for at in spans:
                if l == 0:
                    state = conv[at, :]
                else:
                    state = normed[m, l, at, :]
                centred = state - jnp.sum(state, axis=-1, keepdims=True) * inv_width
                rstd = lax.rsqrt(jnp.sum(centred * centred, axis=-1, keepdims=True) * inv_width + 1e-05)
                norm = centred * rstd
                if l < layers - 1:
                    normed[m, l + 1, at, :] = state
                normed[m, l, at, :] = norm
                inverse[m, l, at, :] = jnp.broadcast_to(rstd, (chunk, LANES))
                padded[pad + at.start : pad + at.stop, :] = norm * gain
            for k in range(3):
                for at in spans:
                    moved = padded[pad + at.start - k * d : pad + at.stop - k * d, :]
                    hidden[m, l, at, k * width : (k + 1) * width] = moved.astype(BF16)
            conv[...] = dot(hidden[m, l], wide[l])
            for at in spans:
                v = conv[at, :]
                v2 = v * v
                t = jnp.tanh(v * (k0 + (k0 * 0.044715) * v2))
                side = 0.5 + 0.5 * t
                slope[m, l, at, :] = side + v * (0.5 - 0.5 * t * t) * (k0 + (3 * k0 * 0.044715) * v2)
                if l < layers - 1:
                    state = normed[m, l + 1, at, :]
                    normed[m, l + 1, at, :] = (state + v * side).astype(BF16).astype(F32)

    def backward(m, after):
        for l in reversed(range(layers)):
            d = 2**l
            gain = gain_ref[l : l + 1, :]
            src = up_ref if l == layers - 1 else grad_ref
            for at in spans:
                padded[pad + at.start : pad + at.stop, :] = src[m, at, :].astype(F32) * slope[m, l, at, :]
            for k in range(3):
                for at in spans:
                    moved = padded[pad + at.start + k * d : pad + at.stop + k * d, :]
                    dwide[m, at, k * width : (k + 1) * width] = moved.astype(BF16)
            for k in range(3):
                part = dot(hidden[m, l, :, 0:width], dwide[m, :, k * width : (k + 1) * width], TN)
                taken = slice(k * width, (k + 1) * width)
                if m == 0:
                    dweight_ref[l, taken, :] = part
                else:
                    dweight_ref[l, taken, :] += part
            dh = dot(dwide[m, :, 0:width], wide[l, 0:width, :], NT)
            dh = dh + dot(dwide[m, :, width : 2 * width], wide[l, width : 2 * width, :], NT)
            dh = dh + dot(dwide[m, :, 2 * width :], wide[l, 2 * width :, :], NT)
            conv[...] = dh
            dgain = jnp.zeros((1, width), F32)
            for at in spans:
                dh = conv[at, :]
                norm = normed[m, l, at, :]
                both = dh * norm
                dgain = dgain + jnp.sum(both, axis=0, keepdims=True)
                dn = dh * gain
                m1 = jnp.sum(dn, axis=-1, keepdims=True) * inv_width
                m2 = jnp.sum(both * gain, axis=-1, keepdims=True) * inv_width
                rstd = inverse[m, l, at, 0:1]
                grad_ref[m, at, :] = (
                    src[m, at, :].astype(F32) + rstd * (dn - m1 - norm * m2)
                ).astype(BF16)
            if m == 0:
                g0[0, l : l + 1, :] = dgain
            else:
                g0[0, l : l + 1, :] += dgain
            after(l)

    def send_back(m):
        for s in range(0, slots, LANES):
            back[m, s : s + LANES, :] = dot(place[m, s : s + LANES, :], grad_ref[m]).astype(BF16)
        pltpu.make_async_copy(back.at[m, here], returned.at[m, here], recv_sem.at[3 + m]).start()
        scatter_to(
            shards - 1,
            device,
            lambda k: back.at[m, pl.ds(pl.multiple_of(index(k) * CAP, CAP), CAP)],
            returned.at[m, here],
            send_sem.at[3 + m],
            recv_sem.at[3 + m],
        )

    theirs = pl.ds(pl.multiple_of((1 - c) * half, half), half)
    ours = pl.ds(pl.multiple_of(c * half, half), half)

    def halves(l):
        s0[l] = dweight_ref[l, theirs, :].astype(BF16)
        if l % deep == 0:
            b = l // deep
            remote(s0.at[pl.ds(l, deep)], r0.at[pl.ds(l, deep)], wsend.at[0, b], wrecv.at[0, b], sibling).start()

    whole(fetched.at[0], recv_sem.at[1])
    forward(0)
    g0[0] = jnp.zeros_like(g0[0])
    backward(0, lambda l: None)
    send_back(0)
    whole(fetched.at[1], recv_sem.at[2])
    forward(1)
    backward(1, halves)
    send_back(1)

    last = batches
    gain_pair = remote(g0.at[0], g0.at[1], wsend.at[0, last], wrecv.at[0, last], sibling)
    gain_pair.start()

    def piece(p):
        return (
            pl.ds(pl.multiple_of((p // 2) * high, 16), high),
            pl.ds(pl.multiple_of(lax.rem(p, 2) * LANES, LANES), LANES),
        )

    def out_piece(p):
        return (
            pl.ds(pl.multiple_of(c * half + (p // 2) * high, 16), high),
            pl.ds(pl.multiple_of(lax.rem(p, 2) * LANES, LANES), LANES),
        )

    order = list(reversed(range(batches)))
    for b in order:
        at = pl.ds(b * deep, deep)
        whole(r0.at[at], wrecv.at[0, b])
        for l in range(b * deep, (b + 1) * deep):
            s1[l] = (dweight_ref[l, ours, :] + r0[l].astype(F32)).astype(BF16)
        pltpu.make_async_copy(s1.at[(at, *piece(p_me))], r1.at[b, p_me], wrecv.at[1, b]).start()
        scatter_to(
            plane - 1,
            p_device,
            lambda k, at=at: s1.at[(at, *piece(p_index(k)))],
            r1.at[b, p_me],
            wsend.at[1, b],
            wrecv.at[1, b],
        )
    gain_pair.wait_recv()
    g1[p_me] = g0[0] + g0[1]
    scatter_to(plane - 1, p_device, lambda k: g1.at[p_me], g1.at[p_me], wsend.at[1, last], wrecv.at[1, last])
    for b in order:
        whole(r1.at[b], wrecv.at[1, b])
        total = r1[b, 0].astype(F32)
        for p in range(1, plane):
            total = total + r1[b, p].astype(F32)
        r2[b, z] = total.astype(BF16)
        scatter_to(z_size - 1, z_device, lambda k, b=b: r2.at[b, z], r2.at[b, z], wsend.at[2, b], wrecv.at[2, b])
    whole(g1.at[pl.ds(0, plane - 1)], wrecv.at[1, last])
    whole(g1.at[pl.ds(0, plane - 1)], wsend.at[1, last])
    total = g1[0]
    for p in range(1, plane):
        total = total + g1[p]
    g2[z] = total
    scatter_to(z_size - 1, z_device, lambda k: g2.at[z], g2.at[z], wsend.at[2, last], wrecv.at[2, last])
    whole(returned.at[0], recv_sem.at[3])
    conv[...] = dot(add[0], returned[0])
    for b in order:
        at = pl.ds(b * deep, deep)
        whole(r2.at[b, pl.ds(0, z_size - 1)], wrecv.at[2, b])
        total = r2[b, 0].astype(F32)
        for k in range(1, z_size):
            total = total + r2[b, k].astype(F32)
        r3[b] = total.astype(BF16)
        mine = weight_out.at[(at, *out_piece(p_me))]
        pltpu.make_async_copy(r3.at[b], mine, wrecv.at[3, b]).start()
        scatter_to(plane - 1, p_device, lambda k, b=b: r3.at[b], mine, wsend.at[3, b], wrecv.at[3, b])

    share = rows // x_size
    whole(returned.at[1], recv_sem.at[4])
    tsend[...] = (conv[0:rows, :] + dot(add[1], returned[1])).astype(BF16).reshape(x_size, share, width)
    pltpu.make_async_copy(tsend.at[x], trecv.at[x], recv_sem.at[5]).start()
    scatter_to(x_size - 1, x_device, lambda k: tsend.at[x_index(k)], trecv.at[x], send_sem.at[5], recv_sem.at[5])

    for b in order:
        at = pl.ds(b * deep, deep)
        done = weight_out.at[at, ours]
        whole(done, wrecv.at[3, b])
        remote(done, done, wsend.at[4, b], wrecv.at[4, b], sibling).start()

    whole(trecv, recv_sem.at[5])
    total = trecv[0].astype(F32)
    for k in range(1, x_size):
        total = total + trecv[k].astype(F32)
    table_out[x] = total.astype(BF16)
    scatter_to(x_size - 1, x_device, lambda k: table_out.at[x], table_out.at[x], send_sem.at[6], recv_sem.at[6])

    whole(g2.at[pl.ds(0, z_size - 1)], wrecv.at[2, last])
    total = g2[0]
    for k in range(1, z_size):
        total = total + g2[k]
    gain_out[...] = total[:layers]
    for b in order:
        whole(weight_out.at[pl.ds(b * deep, deep), theirs], wrecv.at[4, b])
    whole(table_out.at[pl.ds(0, x_size - 1)], recv_sem.at[6])

    whole(ask.at[pl.ds(0, shards - 1)], send_sem.at[0])
    for m in range(MB):
        whole(serve.at[m, pl.ds(0, slots - CAP)], send_sem.at[1 + m])
        whole(back.at[m, pl.ds(0, slots - CAP)], send_sem.at[3 + m])
    whole(tsend.at[pl.ds(0, x_size - 1)], send_sem.at[5])
    whole(tsend.at[pl.ds(0, x_size - 1)], send_sem.at[6])
    for b in range(batches):
        at = pl.ds(b * deep, deep)
        whole(s0.at[at], wsend.at[0, b])
        whole(r1.at[b, pl.ds(0, plane - 1)], wsend.at[1, b])
        whole(r2.at[b, pl.ds(0, z_size - 1)], wsend.at[2, b])
        whole(r1.at[b, pl.ds(0, plane - 1)], wsend.at[3, b])
        whole(weight_out.at[at, ours], wsend.at[4, b])
    gain_pair.wait_send()
    whole(g2.at[pl.ds(0, z_size - 1)], wsend.at[2, last])


def body(table, owner, row, conv_weight, gain, upstream):
    shards, seq_axis = lax.axis_size("emb"), lax.axis_size("seq")
    _, tokens = row.shape
    rows, width = table.shape
    layers, taps, _ = conv_weight.shape
    slots = shards * CAP
    z_size, y_size, _, x_size = plan(shards, seq_axis)
    plane = x_size * y_size
    shape = jax.ShapeDtypeStruct
    dma = pltpu.SemaphoreType.DMA
    half = taps // 2
    high = half // (plane // 2)
    share = rows // x_size
    near = pl.BlockSpec(memory_space=pltpu.VMEM)
    far = pl.BlockSpec(memory_space=pl.ANY)
    weight_sum, gain_sum, table_grad = pl.pallas_call(
        functools.partial(window_kernel, shards, seq_axis, 64),
        out_shape=[
            shape((layers, taps, width), BF16),
            shape((layers, width), F32),
            shape((x_size, share, width), BF16),
        ],
        in_specs=[near, near, near, near, far, far],
        out_specs=[near, near, near],
        scratch_shapes=[
            pltpu.VMEM((shards, MB, LANES), I32),
            pltpu.VMEM((shards, MB, LANES), I32),
            pltpu.VMEM((MB, slots, width), BF16),
            pltpu.VMEM((MB, slots, width), BF16),
            pltpu.VMEM((MB, slots, width), BF16),
            pltpu.VMEM((MB, slots, width), BF16),
            pltpu.VMEM((MB, tokens, slots), BF16),
            pltpu.VMEM((MB, slots, tokens), BF16),
            pltpu.VMEM((MB, rows, slots), BF16),
            pltpu.VMEM((layers, taps, width), F32),
            pltpu.VMEM((MB, tokens, width), BF16),
            pltpu.VMEM((layers, taps, width), BF16),
            pltpu.VMEM((tokens + 32, width), F32),
            pltpu.VMEM((max(tokens, rows), width), F32),
            pltpu.VMEM((MB, layers, tokens, width), F32),
            pltpu.VMEM((MB, layers, tokens, LANES), F32),
            pltpu.VMEM((MB, layers, tokens, width), F32),
            pltpu.VMEM((MB, layers, tokens, taps), BF16),
            pltpu.VMEM((MB, tokens, taps), BF16),
            pltpu.VMEM((MB, tokens, width), BF16),
            pltpu.VMEM((layers, taps, width), F32),
            pltpu.VMEM((x_size, share, width), BF16),
            pltpu.VMEM((x_size, share, width), BF16),
            pltpu.VMEM((layers, half, width), BF16),
            pltpu.VMEM((layers, half, width), BF16),
            pltpu.VMEM((layers, half, width), BF16),
            pltpu.VMEM((2, plane, layers // 2, high, LANES), BF16),
            pltpu.VMEM((2, z_size, layers // 2, high, LANES), BF16),
            pltpu.VMEM((2, layers // 2, high, LANES), BF16),
            pltpu.VMEM((2, 2 * layers, width), F32),
            pltpu.VMEM((plane, 2 * layers, width), F32),
            pltpu.VMEM((z_size, 2 * layers, width), F32),
            dma((2,)),
            dma((7,)),
            dma((7,)),
            dma((5, 3)),
            dma((5, 3)),
        ],
        compiler_params=pltpu.CompilerParams(
            collective_id=0, has_side_effects=True, vmem_limit_bytes=60 * 2**20
        ),
    )(owner.reshape(MB, 1, tokens), row, table, gain, conv_weight, upstream)
    scale = float(MB * tokens * shards * seq_axis) ** (-0.5)
    return weight_sum.astype(F32) * scale, gain_sum * scale, table_grad.astype(F32).reshape(rows, width)


def solution(mesh):
    in_specs = (
        P("emb", None),
        P(("emb", "seq"), None, None),
        P(("emb", "seq"), None),
        P(),
        P(),
        P(("emb", "seq"), None, None),
    )
    out_specs = (P(), P(), P("emb", None))
    return jax.shard_map(body, mesh=mesh, in_specs=in_specs, out_specs=out_specs, check_vma=False)
```

```python
import functools
import math

import jax
import jax.numpy as jnp
from jax import lax
from jax.experimental import pallas as pl
from jax.experimental.pallas import tpu as pltpu
from jax.sharding import PartitionSpec as P

MB = 2
CAP = 16
LANES = 128
F32 = jnp.float32
BF16 = jnp.bfloat16
I32 = jnp.int32
NT = (((1,), (1,)), ((), ()))
TN = (((0,), (0,)), ((), ()))


def plan(shards, seq_axis):
    core = 2
    y = 4 if shards >= 64 else 2
    return shards // (core * y), y, core, seq_axis


def iota(shape, axis):
    return lax.broadcasted_iota(I32, shape, axis)


def dot(a, b, dims=(((1,), (0,)), ((), ()))):
    return lax.dot_general(a, b, dims, preferred_element_type=F32)


def whole(ref, sem):
    pltpu.make_async_copy(ref, ref, sem).wait()


def greet(peers):
    barrier = pltpu.get_barrier_semaphore()
    total = 0
    for count, device in peers:

        def hello(k, carry, device=device):
            pl.semaphore_signal(barrier, inc=1, device_id=device(k), device_id_type=pl.DeviceIdType.MESH)
            return carry

        lax.fori_loop(0, count, hello, 0)
        total += count
    return total


def scatter_to(count, device, src, dst, send_sem, recv_sem):
    def step(k, carry):
        pltpu.make_async_remote_copy(
            src_ref=src(k),
            dst_ref=dst,
            send_sem=send_sem,
            recv_sem=recv_sem,
            device_id=device(k),
            device_id_type=pl.DeviceIdType.MESH,
        ).start()
        return carry

    lax.fori_loop(0, count, step, 0)


def emb_peer(shards):
    me, x = lax.axis_index("emb"), lax.axis_index("seq")

    def index(k):
        return lax.rem(me + k + 1, shards)

    return index, lambda k: (index(k), x)


def to_emb(sizes, src, dst, send_sem, recv_sem, rounds=None):
    z_size, y_size, core, _ = sizes
    line = y_size * core
    me, x = lax.axis_index("emb"), lax.axis_index("seq")
    c, y, z = lax.rem(me, core), lax.rem(me // core, y_size), me // line
    steps = sorted(range(-((z_size - 1) // 2), z_size // 2 + 1), key=lambda d: (-abs(d), -d))
    levels = [lax.rem(z + d + z_size, z_size) * line for d in steps]

    def send(level, near):
        peer = level + near
        pltpu.make_async_remote_copy(
            src_ref=src(peer),
            dst_ref=dst,
            send_sem=send_sem,
            recv_sem=recv_sem,
            device_id=(peer, x),
            device_id_type=pl.DeviceIdType.MESH,
        ).start()

    def step(j, carry):
        k = line - 1 - j
        near = lax.rem(y + k // core, y_size) * core + lax.rem(c + k, core)
        for level in levels:
            send(level, near)
        return carry

    first, last = rounds or (0, line)
    lax.fori_loop(first, min(last, line - 1), step, 0)
    if last == line:
        for level in levels[:-1]:
            send(level, y * core + c)


def requests(owner, row, shards, lane0):
    tokens = owner.shape[1]
    named = iota((shards, tokens), 0) == owner
    marks = jnp.where(named, 1.0, 0.0).astype(F32)
    upto = jnp.where(iota((tokens, tokens), 0) <= iota((tokens, tokens), 1), 1.0, 0.0).astype(BF16)
    ranks = dot(marks.astype(BF16), upto)
    slot = jnp.sum(marks * ranks, axis=0, keepdims=True).astype(I32) - 1
    high = (row // 16).astype(F32)
    low = (row % 16).astype(F32)
    values = jnp.concatenate([marks * high, marks * low], axis=0).astype(BF16)
    places = jnp.where(iota((LANES, tokens), 0) == slot + lane0, 1.0, 0.0).astype(BF16)
    wanted = dot(values, places, NT)
    wanted = wanted[:shards] * 16.0 + wanted[shards:]
    return owner * CAP + slot, wanted.astype(I32)


DURING = {0: [(0, 0)], 1: [(0, 1), (1, 0)], 2: [(1, 1), (2, 0)], 3: [(2, 1), (3, 0), (0, 2)]}
AFTER = [
    [(3, 1), (1, 2)],
    [(2, 2), (0, 3)],
    [(3, 2), (1, 3), (2, 3)],
    [(0, 4), (3, 3), (1, 4)],
]
LATE = [(2, 4), (3, 4), (0, 5), (1, 5)]
LAST = [(2, 5), (3, 5)]


def batches_of(layers):
    return [(l, 1) for l in reversed(range(layers))]


def window_kernel(shards, seq_axis, chunk,
                  owner_ref, row_ref, table_ref, gain_ref, weight_hbm, up_hbm,
                  weight_out, gain_out, table_out,
                  ask, asked, serve, fetched, back, returned, pick, place, add,
                  weight_ref, up_ref, wide, padded, conv, normed, inverse, slope, hidden, dwide, grad_ref,
                  dweight_ref, tsend, trecv, s0, r0, s1, g0, g1, g2, g3,
                  load_sem, send_sem, recv_sem, wsend, wrecv, *work):
    sizes = plan(shards, seq_axis)
    z_size, y_size, _, x_size = sizes
    layers, taps, width = weight_ref.shape
    tokens = row_ref.shape[1]
    rows = table_ref.shape[0]
    slots = shards * CAP
    groups = shards // 8
    e, x = lax.axis_index("emb"), lax.axis_index("seq")
    c = lax.rem(e, 2)
    y = lax.rem(e // 2, y_size)
    z = e // (2 * y_size)
    _, device = emb_peer(shards)
    sibling = (e + 1 - 2 * c, x)
    half = taps // 2
    sets = batches_of(layers)
    count = len(sets)
    r1, s2, r2, t2, r3 = (work[k * count : (k + 1) * count] for k in range(5))
    plane = x_size * y_size
    p_me = x * y_size + y
    high = half // (plane // 2)

    def x_index(k):
        return lax.rem(x + k + 1, x_size)

    def x_device(k):
        return (e, x_index(k))

    def y_index(k):
        return lax.rem(y + k + 1, y_size)

    def y_device(k):
        return ((z * y_size + y_index(k)) * 2 + c, x)

    def p_index(k):
        return lax.rem(p_me + k + 1, plane)

    def p_device(k):
        p = p_index(k)
        return ((z * y_size + lax.rem(p, y_size)) * 2 + c, p // y_size)

    def off_device(k):
        py = lax.rem(y + 1 + lax.rem(k, y_size - 1), y_size)
        px = lax.rem(x + 1 + k // (y_size - 1), x_size)
        return ((z * y_size + py) * 2 + c, px)

    def z_index(k):
        return lax.rem(z + k + 1, z_size)

    def z_device(k):
        return ((z_index(k) * y_size + y) * 2 + c, x)

    def remote(src, dst, send, recv, to):
        return pltpu.make_async_remote_copy(
            src_ref=src, dst_ref=dst, send_sem=send, recv_sem=recv, device_id=to, device_id_type=pl.DeviceIdType.MESH
        )

    load_weight = pltpu.make_async_copy(weight_hbm, weight_ref, load_sem.at[0])
    load_up = pltpu.make_async_copy(up_hbm, up_ref, load_sem.at[1])
    load_weight.start()
    load_up.start()
    expected = greet([(shards - 1, device), (x_size - 1, x_device), ((x_size - 1) * (y_size - 1), off_device)])

    lane0 = lax.rem(e, 8) * CAP
    places = []
    for m in range(MB):
        q, wanted = requests(owner_ref[m], row_ref[m : m + 1, :], shards, lane0)
        ask[:, m, :] = wanted
        places.append(q)
    pl.semaphore_wait(pltpu.get_barrier_semaphore(), expected)
    pltpu.make_async_copy(ask.at[e], asked.at[e], recv_sem.at[0]).start()
    to_emb(sizes, lambda peer: ask.at[peer], asked.at[e], send_sem.at[0], recv_sem.at[0])

    for m in range(MB):
        column = jnp.broadcast_to(places[m].astype(F32), (LANES, tokens)).T
        for s in range(0, slots, LANES):
            pick[m, :, s : s + LANES] = jnp.where(
                column == (iota((tokens, LANES), 1) + s).astype(F32), 1.0, 0.0
            ).astype(BF16)
            place[m, s : s + LANES, :] = jnp.where(iota((LANES, tokens), 0) + s == places[m], 1.0, 0.0).astype(BF16)
    load_weight.wait()
    for l in range(layers):
        wide[l] = weight_ref[l].astype(BF16)
    pad = (padded.shape[0] - tokens) // 2
    padded[0:pad, :] = jnp.zeros((pad, width), F32)
    padded[pad + tokens :, :] = jnp.zeros((pad, width), F32)

    here = pl.ds(pl.multiple_of(e * CAP, CAP), CAP)
    whole(asked, recv_sem.at[0])
    wanted = []
    for m in range(MB):
        ids = jnp.sum(asked[:, m, :].reshape(groups, 8, LANES), axis=1)
        wanted.append(ids)
        tall = jnp.concatenate([ids.astype(F32)] * (LANES // groups), axis=0).T
        for g in range(groups):
            hot = jnp.where(iota((LANES, rows), 1).astype(F32) == tall[:, g : g + 1], 1.0, 0.0).astype(BF16)
            serve[m, g * LANES : (g + 1) * LANES, :] = dot(hot, table_ref[...]).astype(BF16)
        pltpu.make_async_copy(serve.at[m, here], fetched.at[m, here], recv_sem.at[1 + m]).start()
        to_emb(
            sizes,
            lambda peer, m=m: serve.at[m, pl.ds(pl.multiple_of(peer * CAP, CAP), CAP)],
            fetched.at[m, here],
            send_sem.at[1 + m],
            recv_sem.at[1 + m],
        )
    for m in range(MB):
        for g in range(groups):
            add[m, :, g * LANES : (g + 1) * LANES] = jnp.where(
                iota((rows, LANES), 0) == wanted[m][g : g + 1, :], 1.0, 0.0
            ).astype(BF16)
    load_up.wait()

    spans = [slice(at, at + chunk) for at in range(0, tokens, chunk)]
    inv_width = 1.0 / width
    k0 = math.sqrt(2.0 / math.pi)

    def forward(m):
        conv[...] = dot(pick[m], fetched[m])
        for l in range(layers):
            d = 2**l
            gain = gain_ref[l : l + 1, :]
            for at in spans:
                if l == 0:
                    state = conv[at, :]
                else:
                    state = normed[m, l, at, :]
                centred = state - jnp.sum(state, axis=-1, keepdims=True) * inv_width
                rstd = lax.rsqrt(jnp.sum(centred * centred, axis=-1, keepdims=True) * inv_width + 1e-05)
                norm = centred * rstd
                if l < layers - 1:
                    normed[m, l + 1, at, :] = state
                normed[m, l, at, :] = norm
                inverse[m, l, at, :] = jnp.broadcast_to(rstd, (chunk, LANES))
                padded[pad + at.start : pad + at.stop, :] = norm * gain
            for k in range(3):
                for at in spans:
                    moved = padded[pad + at.start - k * d : pad + at.stop - k * d, :]
                    hidden[m, l, at, k * width : (k + 1) * width] = moved.astype(BF16)
            conv[...] = dot(hidden[m, l], wide[l])
            for at in spans:
                v = conv[at, :]
                v2 = v * v
                t = jnp.tanh(v * (k0 + (k0 * 0.044715) * v2))
                side = 0.5 + 0.5 * t
                slope[m, l, at, :] = side + v * (0.5 - 0.5 * t * t) * (k0 + (3 * k0 * 0.044715) * v2)
                if l < layers - 1:
                    state = normed[m, l + 1, at, :]
                    normed[m, l + 1, at, :] = (state + v * side).astype(BF16).astype(F32)

    def backward(m, after):
        for l in reversed(range(layers)):
            d = 2**l
            gain = gain_ref[l : l + 1, :]
            src = up_ref if l == layers - 1 else grad_ref
            for at in spans:
                padded[pad + at.start : pad + at.stop, :] = src[m, at, :].astype(F32) * slope[m, l, at, :]
            for k in range(3):
                for at in spans:
                    moved = padded[pad + at.start + k * d : pad + at.stop + k * d, :]
                    dwide[m, at, k * width : (k + 1) * width] = moved.astype(BF16)
            for k in range(3):
                part = dot(hidden[m, l, :, 0:width], dwide[m, :, k * width : (k + 1) * width], TN)
                taken = slice(k * width, (k + 1) * width)
                if m == 0:
                    dweight_ref[l, taken, :] = part
                else:
                    dweight_ref[l, taken, :] += part
            dh = dot(dwide[m, :, 0:width], wide[l, 0:width, :], NT)
            dh = dh + dot(dwide[m, :, width : 2 * width], wide[l, width : 2 * width, :], NT)
            dh = dh + dot(dwide[m, :, 2 * width :], wide[l, 2 * width :, :], NT)
            conv[...] = dh
            dgain = jnp.zeros((1, width), F32)
            for at in spans:
                dh = conv[at, :]
                norm = normed[m, l, at, :]
                both = dh * norm
                dgain = dgain + jnp.sum(both, axis=0, keepdims=True)
                dn = dh * gain
                m1 = jnp.sum(dn, axis=-1, keepdims=True) * inv_width
                m2 = jnp.sum(both * gain, axis=-1, keepdims=True) * inv_width
                rstd = inverse[m, l, at, 0:1]
                grad_ref[m, at, :] = (
                    src[m, at, :].astype(F32) + rstd * (dn - m1 - norm * m2)
                ).astype(BF16)
            if m == 0:
                g0[0, l : l + 1, :] = dgain
            else:
                g0[0, l : l + 1, :] += dgain
            after(l)

    def line_up(m):
        for s in range(0, slots, LANES):
            back[m, s : s + LANES, :] = dot(place[m, s : s + LANES, :], grad_ref[m]).astype(BF16)
        pltpu.make_async_copy(back.at[m, here], returned.at[m, here], recv_sem.at[3 + m]).start()

    def send_back(m, rounds=None):
        to_emb(
            sizes,
            lambda peer: back.at[m, pl.ds(pl.multiple_of(peer * CAP, CAP), CAP)],
            returned.at[m, here],
            send_sem.at[3 + m],
            recv_sem.at[3 + m],
            rounds,
        )

    theirs = pl.ds(pl.multiple_of((1 - c) * half, half), half)
    ours = pl.ds(pl.multiple_of(c * half, half), half)


    def of(b):
        return pl.ds(sets[b][0], sets[b][1])

    def piece(b, p, start):
        return (
            of(b),
            pl.ds(pl.multiple_of(start + (p // 2) * high, 16), high),
            pl.ds(pl.multiple_of(lax.rem(p, 2) * LANES, LANES), LANES),
        )

    def added(ref, size):
        total = ref[0].astype(F32)
        for k in range(1, size):
            total = total + ref[k].astype(F32)
        return total

    def pair(b):
        for l in range(sets[b][0], sum(sets[b])):
            s0[l] = dweight_ref[l, theirs, :].astype(BF16)
        remote(s0.at[of(b)], r0.at[of(b)], wsend.at[0, b], wrecv.at[0, b], sibling).start()

    def across(b):
        whole(r0.at[of(b)], wrecv.at[0, b])
        for l in range(sets[b][0], sum(sets[b])):
            s1[l] = (dweight_ref[l, ours, :] + r0[l].astype(F32)).astype(BF16)
        pltpu.make_async_copy(s1.at[piece(b, p_me, 0)], r1[b].at[p_me], wrecv.at[1, b]).start()
        scatter_to(
            plane - 1, p_device, lambda k: s1.at[piece(b, p_index(k), 0)], r1[b].at[p_me], wsend.at[1, b], wrecv.at[1, b]
        )

    def along(b):
        whole(r1[b], wrecv.at[1, b])
        total = added(r1[b], plane)
        total = total.reshape(total.shape[0] * total.shape[1], LANES)
        per = total.shape[0] // z_size
        for k in range(z_size):
            s2[b][k, 0:per, :] = total[k * per : (k + 1) * per].astype(BF16)
        pltpu.make_async_copy(s2[b].at[z], r2[b].at[z], wrecv.at[2, b]).start()
        scatter_to(z_size - 1, z_device, lambda k: s2[b].at[z_index(k)], r2[b].at[z], wsend.at[2, b], wrecv.at[2, b])

    def told(b):
        whole(r2[b], wrecv.at[2, b])
        t2[b][z] = added(r2[b], z_size).astype(BF16)
        scatter_to(z_size - 1, z_device, lambda k: t2[b].at[z], t2[b].at[z], wsend.at[5, b], wrecv.at[5, b])

    def across_back(b):
        whole(t2[b].at[pl.ds(0, z_size - 1)], wrecv.at[5, b])
        per = r3[b].shape[0] * r3[b].shape[1] // z_size
        total = jnp.concatenate([t2[b][k, 0:per, :].astype(F32) for k in range(z_size)], axis=0)
        r3[b][...] = total.reshape(r3[b].shape).astype(BF16)
        spot = weight_out.at[piece(b, p_me, c * half)]
        pltpu.make_async_copy(r3[b], spot, wrecv.at[3, b]).start()
        scatter_to(plane - 1, p_device, lambda k: r3[b], spot, wsend.at[3, b], wrecv.at[3, b])

    def pair_back(b):
        done = weight_out.at[of(b), ours]
        whole(done, wrecv.at[3, b])
        remote(done, done, wsend.at[4, b], wrecv.at[4, b], sibling).start()

    way = [pair, across, along, told, across_back, pair_back]

    def advance(*steps):
        for b, phase in steps:
            way[phase](b)

    def gain_axis(phase, me, size, to, source, ref):
        ref[me] = source
        scatter_to(size - 1, to, lambda k: ref.at[me], ref.at[me], wsend.at[phase, count], wrecv.at[phase, count])

    def gain_sum(phase, size, ref):
        whole(ref.at[pl.ds(0, size - 1)], wrecv.at[phase, count])
        return added(ref, size)

    def during(l):
        for step in DURING.get(layers - 1 - l, ()):
            advance(step)

    whole(fetched.at[0], recv_sem.at[1])
    forward(0)
    g0[0] = jnp.zeros_like(g0[0])
    backward(0, lambda l: None)
    line_up(0)
    send_back(0)
    whole(fetched.at[1], recv_sem.at[2])
    forward(1)
    backward(1, during)

    gain_pair = remote(g0.at[0], g0.at[1], wsend.at[0, count], wrecv.at[0, count], sibling)
    gain_pair.start()
    line_up(1)
    parts = len(AFTER)
    cuts = [2 * y_size * k // parts for k in range(parts + 1)]
    for k, steps in enumerate(AFTER):
        send_back(1, (cuts[k], cuts[k + 1]))
        advance(*steps)
        if k == 0:
            gain_pair.wait_recv()
            gain_axis(1, x, x_size, x_device, g0[0] + g0[1], g1)
        if k == 1:
            gain_axis(2, y, y_size, y_device, gain_sum(1, x_size, g1), g2)
        if k == 2:
            gain_axis(3, z, z_size, z_device, gain_sum(2, y_size, g2), g3)
    whole(returned.at[0], recv_sem.at[3])
    conv[0:rows, :] = dot(add[0], returned[0])
    advance(*LATE)

    share = rows // x_size
    whole(returned.at[1], recv_sem.at[4])
    tsend[...] = (conv[0:rows, :] + dot(add[1], returned[1])).astype(BF16).reshape(x_size, share, width)
    pltpu.make_async_copy(tsend.at[x], trecv.at[x], recv_sem.at[5]).start()
    scatter_to(x_size - 1, x_device, lambda k: tsend.at[x_index(k)], trecv.at[x], send_sem.at[5], recv_sem.at[5])
    advance(*LAST)
    whole(trecv, recv_sem.at[5])
    table_out[x] = added(trecv, x_size).astype(BF16)
    scatter_to(x_size - 1, x_device, lambda k: table_out.at[x], table_out.at[x], send_sem.at[6], recv_sem.at[6])

    gain_out[...] = gain_sum(3, z_size, g3)
    for b in range(count):
        whole(weight_out.at[of(b), theirs], wrecv.at[4, b])
    whole(table_out.at[pl.ds(0, x_size - 1)], recv_sem.at[6])

    whole(ask.at[pl.ds(0, shards - 1)], send_sem.at[0])
    for m in range(MB):
        whole(serve.at[m, pl.ds(0, slots - CAP)], send_sem.at[1 + m])
        whole(back.at[m, pl.ds(0, slots - CAP)], send_sem.at[3 + m])
    whole(tsend.at[pl.ds(0, x_size - 1)], send_sem.at[5])
    whole(tsend.at[pl.ds(0, x_size - 1)], send_sem.at[6])
    for b in range(count):
        whole(s0.at[of(b)], wsend.at[0, b])
        whole(r1[b].at[pl.ds(0, plane - 1)], wsend.at[1, b])
        whole(s2[b].at[pl.ds(0, z_size - 1)], wsend.at[2, b])
        whole(t2[b].at[pl.ds(0, z_size - 1)], wsend.at[5, b])
        whole(r1[b].at[pl.ds(0, plane - 1)], wsend.at[3, b])
        whole(weight_out.at[of(b), ours], wsend.at[4, b])
    gain_pair.wait_send()
    whole(g1.at[pl.ds(0, x_size - 1)], wsend.at[1, count])
    whole(g2.at[pl.ds(0, y_size - 1)], wsend.at[2, count])
    whole(g3.at[pl.ds(0, z_size - 1)], wsend.at[3, count])


def scale_kernel(scale, weight_ref, gain_ref, table_ref, weight_out, gain_out, table_out,
                 weight, wide, table, tall, load_sem, store_sem):
    layers = weight.shape[0]
    loads = [pltpu.make_async_copy(weight_ref.at[l], weight.at[l], load_sem.at[l]) for l in range(layers)]
    loads.append(pltpu.make_async_copy(table_ref, table, load_sem.at[layers]))
    stores = [pltpu.make_async_copy(wide.at[l], weight_out.at[l], store_sem.at[l]) for l in range(layers)]
    stores.append(pltpu.make_async_copy(tall, table_out, store_sem.at[layers]))
    for load in loads:
        load.start()
    gain_out[...] = gain_ref[...] * scale
    for l in range(layers):
        loads[l].wait()
        wide[l] = weight[l].astype(F32) * scale
        stores[l].start()
    loads[layers].wait()
    tall[...] = table[...].astype(F32)
    stores[layers].start()
    for store in stores:
        store.wait()


def body(table, owner, row, conv_weight, gain, upstream):
    shards, seq_axis = lax.axis_size("emb"), lax.axis_size("seq")
    _, tokens = row.shape
    rows, width = table.shape
    layers, taps, _ = conv_weight.shape
    slots = shards * CAP
    z_size, y_size, _, x_size = plan(shards, seq_axis)
    sets = batches_of(layers)
    shape = jax.ShapeDtypeStruct
    dma = pltpu.SemaphoreType.DMA
    half = taps // 2
    share = rows // x_size
    plane = x_size * y_size
    high = half // (plane // 2)
    one_z = [(z_size, -(-n * high // z_size // 16) * 16, LANES) for _, n in sets]
    shapes = (
        [(plane, n, high, LANES) for _, n in sets]
        + one_z * 3
        + [(n, high, LANES) for _, n in sets]
    )
    work = [pltpu.VMEM(dims, BF16) for dims in shapes]
    near = pl.BlockSpec(memory_space=pltpu.VMEM)
    far = pl.BlockSpec(memory_space=pl.ANY)
    weight_sum, gain_sum, table_grad = pl.pallas_call(
        functools.partial(window_kernel, shards, seq_axis, 64),
        out_shape=[
            shape((layers, taps, width), BF16),
            shape((layers, width), F32),
            shape((x_size, share, width), BF16),
        ],
        in_specs=[near, near, near, near, far, far],
        out_specs=[near, near, near],
        scratch_shapes=[
            pltpu.VMEM((shards, MB, LANES), I32),
            pltpu.VMEM((shards, MB, LANES), I32),
            pltpu.VMEM((MB, slots, width), BF16),
            pltpu.VMEM((MB, slots, width), BF16),
            pltpu.VMEM((MB, slots, width), BF16),
            pltpu.VMEM((MB, slots, width), BF16),
            pltpu.VMEM((MB, tokens, slots), BF16),
            pltpu.VMEM((MB, slots, tokens), BF16),
            pltpu.VMEM((MB, rows, slots), BF16),
            pltpu.VMEM((layers, taps, width), F32),
            pltpu.VMEM((MB, tokens, width), BF16),
            pltpu.VMEM((layers, taps, width), BF16),
            pltpu.VMEM((tokens + 32, width), F32),
            pltpu.VMEM((max(tokens, rows), width), F32),
            pltpu.VMEM((MB, layers, tokens, width), F32),
            pltpu.VMEM((MB, layers, tokens, LANES), F32),
            pltpu.VMEM((MB, layers, tokens, width), F32),
            pltpu.VMEM((MB, layers, tokens, taps), BF16),
            pltpu.VMEM((MB, tokens, taps), BF16),
            pltpu.VMEM((MB, tokens, width), BF16),
            pltpu.VMEM((layers, taps, width), F32),
            pltpu.VMEM((x_size, share, width), BF16),
            pltpu.VMEM((x_size, share, width), BF16),
            pltpu.VMEM((layers, half, width), BF16),
            pltpu.VMEM((layers, half, width), BF16),
            pltpu.VMEM((layers, half, width), BF16),
            pltpu.VMEM((2, layers, width), F32),
            pltpu.VMEM((x_size, layers, width), F32),
            pltpu.VMEM((y_size, layers, width), F32),
            pltpu.VMEM((z_size, layers, width), F32),
            dma((2,)),
            dma((7,)),
            dma((7,)),
            dma((6, len(sets) + 1)),
            dma((6, len(sets) + 1)),
            *work,
        ],
        compiler_params=pltpu.CompilerParams(
            collective_id=0, has_side_effects=True, vmem_limit_bytes=60 * 2**20
        ),
    )(owner.reshape(MB, 1, tokens), row, table, gain, conv_weight, upstream)
    scale = float(MB * tokens * shards * seq_axis) ** (-0.5)
    return pl.pallas_call(
        functools.partial(scale_kernel, scale),
        out_shape=[shape((layers, taps, width), F32), shape((layers, width), F32), shape((rows, width), F32)],
        in_specs=[far, near, far],
        out_specs=[far, near, far],
        scratch_shapes=[
            pltpu.VMEM((layers, taps, width), BF16),
            pltpu.VMEM((layers, taps, width), F32),
            pltpu.VMEM((rows, width), BF16),
            pltpu.VMEM((rows, width), F32),
            dma((layers + 1,)),
            dma((layers + 1,)),
        ],
        compiler_params=pltpu.CompilerParams(vmem_limit_bytes=60 * 2**20),
    )(weight_sum, gain_sum, table_grad.reshape(rows, width))


def solution(mesh):
    in_specs = (
        P("emb", None),
        P(("emb", "seq"), None, None),
        P(("emb", "seq"), None),
        P(),
        P(),
        P(("emb", "seq"), None, None),
    )
    out_specs = (P(), P(), P("emb", None))
    return jax.shard_map(body, mesh=mesh, in_specs=in_specs, out_specs=out_specs, check_vma=False)
```

```python
import functools
import math

import jax
import jax.numpy as jnp
from jax import lax
from jax.experimental import pallas as pl
from jax.experimental.pallas import tpu as pltpu
from jax.sharding import PartitionSpec as P

MB = 2
CAP = 16
LANES = 128
F32 = jnp.float32
BF16 = jnp.bfloat16
I32 = jnp.int32
NT = (((1,), (1,)), ((), ()))
TN = (((0,), (0,)), ((), ()))


def plan(shards, seq_axis):
    core = 2
    y = 4 if shards >= 64 else 2
    return shards // (core * y), y, core, seq_axis


def iota(shape, axis):
    return lax.broadcasted_iota(I32, shape, axis)


def dot(a, b, dims=(((1,), (0,)), ((), ()))):
    return lax.dot_general(a, b, dims, preferred_element_type=F32)


def whole(ref, sem):
    pltpu.make_async_copy(ref, ref, sem).wait()


def greet(peers):
    barrier = pltpu.get_barrier_semaphore()
    total = 0
    for count, device in peers:

        def hello(k, carry, device=device):
            pl.semaphore_signal(barrier, inc=1, device_id=device(k), device_id_type=pl.DeviceIdType.MESH)
            return carry

        lax.fori_loop(0, count, hello, 0)
        total += count
    return total


def scatter_to(count, device, src, dst, send_sem, recv_sem):
    def step(k, carry):
        pltpu.make_async_remote_copy(
            src_ref=src(k),
            dst_ref=dst,
            send_sem=send_sem,
            recv_sem=recv_sem,
            device_id=device(k),
            device_id_type=pl.DeviceIdType.MESH,
        ).start()
        return carry

    lax.fori_loop(0, count, step, 0)


def emb_peer(shards):
    me, x = lax.axis_index("emb"), lax.axis_index("seq")

    def index(k):
        return lax.rem(me + k + 1, shards)

    return index, lambda k: (index(k), x)


def to_emb(sizes, src, dst, send_sem, recv_sem, rounds=None):
    z_size, y_size, core, _ = sizes
    line = y_size * core
    me, x = lax.axis_index("emb"), lax.axis_index("seq")
    c, y, z = lax.rem(me, core), lax.rem(me // core, y_size), me // line
    steps = sorted(range(-((z_size - 1) // 2), z_size // 2 + 1), key=lambda d: (-abs(d), -d))
    levels = [lax.rem(z + d + z_size, z_size) * line for d in steps]

    def send(level, near):
        peer = level + near
        pltpu.make_async_remote_copy(
            src_ref=src(peer),
            dst_ref=dst,
            send_sem=send_sem,
            recv_sem=recv_sem,
            device_id=(peer, x),
            device_id_type=pl.DeviceIdType.MESH,
        ).start()

    def step(j, carry):
        k = line - 1 - j
        near = lax.rem(y + k // core, y_size) * core + lax.rem(c + k, core)
        for level in levels:
            send(level, near)
        return carry

    first, last = rounds or (0, line)
    lax.fori_loop(first, min(last, line - 1), step, 0)
    if last == line:
        for level in levels[:-1]:
            send(level, y * core + c)


def requests(owner, row, shards, lane0):
    tokens = owner.shape[1]
    named = iota((shards, tokens), 0) == owner
    marks = jnp.where(named, 1.0, 0.0).astype(F32)
    upto = jnp.where(iota((tokens, tokens), 0) <= iota((tokens, tokens), 1), 1.0, 0.0).astype(BF16)
    ranks = dot(marks.astype(BF16), upto)
    slot = jnp.sum(marks * ranks, axis=0, keepdims=True).astype(I32) - 1
    high = (row // 16).astype(F32)
    low = (row % 16).astype(F32)
    values = jnp.concatenate([marks * high, marks * low], axis=0).astype(BF16)
    places = jnp.where(iota((LANES, tokens), 0) == slot + lane0, 1.0, 0.0).astype(BF16)
    wanted = dot(values, places, NT)
    wanted = wanted[:shards] * 16.0 + wanted[shards:]
    return owner * CAP + slot, wanted.astype(I32)


DURING = {0: [(0, 0)], 1: [(0, 1), (1, 0)], 2: [(1, 1), (2, 0)], 3: [(2, 1), (3, 0)]}


def batches_of(layers):
    return [(l, 1) for l in reversed(range(layers))]


def window_kernel(shards, seq_axis, chunk,
                  owner_ref, row_ref, table_ref, gain_ref, weight_hbm, up_hbm,
                  weight_out, gain_out, table_out,
                  ask, asked, serve, fetched, back, returned, pick, place, add,
                  weight_ref, up_ref, wide, padded, conv, normed, inverse, slope, hidden, dwide, grad_ref,
                  dweight_ref, tsend, trecv, s0, r0, s1, g0, g1, g2, g3,
                  load_sem, send_sem, recv_sem, wsend, wrecv, *work):
    sizes = plan(shards, seq_axis)
    z_size, y_size, _, x_size = sizes
    layers, taps, width = weight_ref.shape
    tokens = row_ref.shape[1]
    rows = table_ref.shape[0]
    slots = shards * CAP
    groups = shards // 8
    e, x = lax.axis_index("emb"), lax.axis_index("seq")
    c = lax.rem(e, 2)
    y = lax.rem(e // 2, y_size)
    z = e // (2 * y_size)
    _, device = emb_peer(shards)
    sibling = (e + 1 - 2 * c, x)
    half = taps // 2
    sets = batches_of(layers)
    count = len(sets)
    r1 = work[:count]
    r3, s2, r2, t2 = (work[count + 2 * k : count + 2 * k + 2] for k in range(4))
    plane = x_size * y_size
    p_me = x * y_size + y
    high = half // (plane // 2)

    def x_index(k):
        return lax.rem(x + k + 1, x_size)

    def x_device(k):
        return (e, x_index(k))

    def y_index(k):
        return lax.rem(y + k + 1, y_size)

    def y_device(k):
        return ((z * y_size + y_index(k)) * 2 + c, x)

    def p_index(k):
        return lax.rem(p_me + k + 1, plane)

    def p_device(k):
        p = p_index(k)
        return ((z * y_size + lax.rem(p, y_size)) * 2 + c, p // y_size)

    def off_device(k):
        py = lax.rem(y + 1 + lax.rem(k, y_size - 1), y_size)
        px = lax.rem(x + 1 + k // (y_size - 1), x_size)
        return ((z * y_size + py) * 2 + c, px)

    def z_index(k):
        return lax.rem(z + k + 1, z_size)

    def z_device(k):
        return ((z_index(k) * y_size + y) * 2 + c, x)

    def remote(src, dst, send, recv, to):
        return pltpu.make_async_remote_copy(
            src_ref=src, dst_ref=dst, send_sem=send, recv_sem=recv, device_id=to, device_id_type=pl.DeviceIdType.MESH
        )

    load_weight = pltpu.make_async_copy(weight_hbm, weight_ref, load_sem.at[0])
    load_up = pltpu.make_async_copy(up_hbm, up_ref, load_sem.at[1])
    load_weight.start()
    load_up.start()
    expected = greet([(shards - 1, device), (x_size - 1, x_device), ((x_size - 1) * (y_size - 1), off_device)])

    lane0 = lax.rem(e, 8) * CAP
    places = []
    for m in range(MB):
        q, wanted = requests(owner_ref[m], row_ref[m : m + 1, :], shards, lane0)
        ask[:, m, :] = wanted
        places.append(q)
    pl.semaphore_wait(pltpu.get_barrier_semaphore(), expected)
    pltpu.make_async_copy(ask.at[e], asked.at[e], recv_sem.at[0]).start()
    to_emb(sizes, lambda peer: ask.at[peer], asked.at[e], send_sem.at[0], recv_sem.at[0])

    for m in range(MB):
        column = jnp.broadcast_to(places[m].astype(F32), (LANES, tokens)).T
        for s in range(0, slots, LANES):
            pick[m, :, s : s + LANES] = jnp.where(
                column == (iota((tokens, LANES), 1) + s).astype(F32), 1.0, 0.0
            ).astype(BF16)
            place[m, s : s + LANES, :] = jnp.where(iota((LANES, tokens), 0) + s == places[m], 1.0, 0.0).astype(BF16)
    load_weight.wait()
    for l in range(layers):
        wide[l] = weight_ref[l].astype(BF16)
    pad = (padded.shape[0] - tokens) // 2
    padded[0:pad, :] = jnp.zeros((pad, width), F32)
    padded[pad + tokens :, :] = jnp.zeros((pad, width), F32)

    here = pl.ds(pl.multiple_of(e * CAP, CAP), CAP)
    whole(asked, recv_sem.at[0])
    wanted = []
    for m in range(MB):
        ids = jnp.sum(asked[:, m, :].reshape(groups, 8, LANES), axis=1)
        wanted.append(ids)
        tall = jnp.concatenate([ids.astype(F32)] * (LANES // groups), axis=0).T
        for g in range(groups):
            hot = jnp.where(iota((LANES, rows), 1).astype(F32) == tall[:, g : g + 1], 1.0, 0.0).astype(BF16)
            serve[m, g * LANES : (g + 1) * LANES, :] = dot(hot, table_ref[...]).astype(BF16)
        if m:
            whole(serve.at[0, pl.ds(0, slots - CAP)], send_sem.at[1])
        pltpu.make_async_copy(serve.at[m, here], fetched.at[m, here], recv_sem.at[1 + m]).start()
        to_emb(
            sizes,
            lambda peer, m=m: serve.at[m, pl.ds(pl.multiple_of(peer * CAP, CAP), CAP)],
            fetched.at[m, here],
            send_sem.at[1 + m],
            recv_sem.at[1 + m],
        )
    for m in range(MB):
        for g in range(groups):
            add[m, :, g * LANES : (g + 1) * LANES] = jnp.where(
                iota((rows, LANES), 0) == wanted[m][g : g + 1, :], 1.0, 0.0
            ).astype(BF16)
    load_up.wait()

    spans = [slice(at, at + chunk) for at in range(0, tokens, chunk)]
    inv_width = 1.0 / width
    k0 = math.sqrt(2.0 / math.pi)

    def forward(m):
        conv[...] = dot(pick[m], fetched[m])
        for l in range(layers):
            d = 2**l
            gain = gain_ref[l : l + 1, :]
            for at in spans:
                if l == 0:
                    state = conv[at, :]
                else:
                    state = normed[m, l, at, :]
                centred = state - jnp.sum(state, axis=-1, keepdims=True) * inv_width
                rstd = lax.rsqrt(jnp.sum(centred * centred, axis=-1, keepdims=True) * inv_width + 1e-05)
                norm = centred * rstd
                if l < layers - 1:
                    normed[m, l + 1, at, :] = state
                normed[m, l, at, :] = norm
                inverse[m, l, at, :] = jnp.broadcast_to(rstd, (chunk, LANES))
                padded[pad + at.start : pad + at.stop, :] = norm * gain
            for k in range(3):
                for at in spans:
                    moved = padded[pad + at.start - k * d : pad + at.stop - k * d, :]
                    hidden[m, l, at, k * width : (k + 1) * width] = moved.astype(BF16)
            conv[...] = dot(hidden[m, l], wide[l])
            for at in spans:
                v = conv[at, :]
                v2 = v * v
                t = jnp.tanh(v * (k0 + (k0 * 0.044715) * v2))
                side = 0.5 + 0.5 * t
                slope[m, l, at, :] = side + v * (0.5 - 0.5 * t * t) * (k0 + (3 * k0 * 0.044715) * v2)
                if l < layers - 1:
                    state = normed[m, l + 1, at, :]
                    normed[m, l + 1, at, :] = (state + v * side).astype(BF16).astype(F32)

    def backward(m, after):
        for l in reversed(range(layers)):
            d = 2**l
            gain = gain_ref[l : l + 1, :]
            src = up_ref if l == layers - 1 else grad_ref
            for at in spans:
                padded[pad + at.start : pad + at.stop, :] = src[m, at, :].astype(F32) * slope[m, l, at, :]
            for k in range(3):
                for at in spans:
                    moved = padded[pad + at.start + k * d : pad + at.stop + k * d, :]
                    dwide[m, at, k * width : (k + 1) * width] = moved.astype(BF16)
            for k in range(3):
                part = dot(hidden[m, l, :, 0:width], dwide[m, :, k * width : (k + 1) * width], TN)
                taken = slice(k * width, (k + 1) * width)
                if m == 0:
                    dweight_ref[l, taken, :] = part
                else:
                    dweight_ref[l, taken, :] += part
            dh = dot(dwide[m, :, 0:width], wide[l, 0:width, :], NT)
            dh = dh + dot(dwide[m, :, width : 2 * width], wide[l, width : 2 * width, :], NT)
            dh = dh + dot(dwide[m, :, 2 * width :], wide[l, 2 * width :, :], NT)
            conv[...] = dh
            dgain = jnp.zeros((1, width), F32)
            for at in spans:
                dh = conv[at, :]
                norm = normed[m, l, at, :]
                both = dh * norm
                dgain = dgain + jnp.sum(both, axis=0, keepdims=True)
                dn = dh * gain
                m1 = jnp.sum(dn, axis=-1, keepdims=True) * inv_width
                m2 = jnp.sum(both * gain, axis=-1, keepdims=True) * inv_width
                rstd = inverse[m, l, at, 0:1]
                grad_ref[m, at, :] = (
                    src[m, at, :].astype(F32) + rstd * (dn - m1 - norm * m2)
                ).astype(BF16)
            if m == 0:
                g0[0, l : l + 1, :] = dgain
            else:
                g0[0, l : l + 1, :] += dgain
            after(l)

    def line_up(m):
        for s in range(0, slots, LANES):
            back[m, s : s + LANES, :] = dot(place[m, s : s + LANES, :], grad_ref[m]).astype(BF16)
        pltpu.make_async_copy(back.at[m, here], returned.at[m, here], recv_sem.at[3 + m]).start()

    def send_back(m, rounds=None):
        to_emb(
            sizes,
            lambda peer: back.at[m, pl.ds(pl.multiple_of(peer * CAP, CAP), CAP)],
            returned.at[m, here],
            send_sem.at[3 + m],
            recv_sem.at[3 + m],
            rounds,
        )

    theirs = pl.ds(pl.multiple_of((1 - c) * half, half), half)
    ours = pl.ds(pl.multiple_of(c * half, half), half)


    def of(b):
        return pl.ds(sets[b][0], sets[b][1])

    def piece(some, p, start):
        return (
            some,
            pl.ds(pl.multiple_of(start + (p // 2) * high, 16), high),
            pl.ds(pl.multiple_of(lax.rem(p, 2) * LANES, LANES), LANES),
        )

    def added(ref, size):
        total = ref[0].astype(F32)
        for k in range(1, size):
            total = total + ref[k].astype(F32)
        return total

    def pair(b):
        for l in range(sets[b][0], sum(sets[b])):
            s0[l] = dweight_ref[l, theirs, :].astype(BF16)
        remote(s0.at[of(b)], r0.at[of(b)], wsend.at[0, b], wrecv.at[0, b], sibling).start()

    def across(b):
        whole(r0.at[of(b)], wrecv.at[0, b])
        for l in range(sets[b][0], sum(sets[b])):
            s1[l] = (dweight_ref[l, ours, :] + r0[l].astype(F32)).astype(BF16)
        pltpu.make_async_copy(s1.at[piece(of(b), p_me, 0)], r1[b].at[p_me], wrecv.at[1, b]).start()
        scatter_to(
            plane - 1, p_device, lambda k: s1.at[piece(of(b), p_index(k), 0)], r1[b].at[p_me], wsend.at[1, b], wrecv.at[1, b]
        )

    deep = layers // 2
    per_z = deep * high // z_size

    def along(h):
        parts = []
        for l in range(h * deep, (h + 1) * deep):
            b = layers - 1 - l
            whole(r1[b], wrecv.at[1, b])
            parts.append(added(r1[b], plane).reshape(high, LANES))
        total = jnp.concatenate(parts, axis=0)
        for k in range(z_size):
            s2[h][k, 0:per_z, :] = total[k * per_z : (k + 1) * per_z].astype(BF16)
        pltpu.make_async_copy(s2[h].at[z], r2[h].at[z], wrecv.at[2, h]).start()
        scatter_to(z_size - 1, z_device, lambda k: s2[h].at[z_index(k)], r2[h].at[z], wsend.at[2, h], wrecv.at[2, h])

    def told(h):
        whole(r2[h], wrecv.at[2, h])
        t2[h][z] = added(r2[h], z_size).astype(BF16)
        scatter_to(z_size - 1, z_device, lambda k: t2[h].at[z], t2[h].at[z], wsend.at[5, h], wrecv.at[5, h])

    def across_back(h):
        whole(t2[h].at[pl.ds(0, z_size - 1)], wrecv.at[5, h])
        total = jnp.concatenate([t2[h][k, 0:per_z, :].astype(F32) for k in range(z_size)], axis=0)
        r3[h][...] = total.reshape(deep, high, LANES).astype(BF16)
        spot = weight_out.at[piece(pl.ds(h * deep, deep), p_me, c * half)]
        pltpu.make_async_copy(r3[h], spot, wrecv.at[3, h]).start()
        scatter_to(plane - 1, p_device, lambda k: r3[h], spot, wsend.at[3, h], wrecv.at[3, h])

    def pair_back(h):
        done = weight_out.at[pl.ds(h * deep, deep), ours]
        whole(done, wrecv.at[3, h])
        remote(done, done, wsend.at[4, h], wrecv.at[4, h], sibling).start()

    way = [pair, across]

    def advance(*steps):
        for b, phase in steps:
            way[phase](b)

    def gain_axis(phase, me, size, to, source, ref):
        ref[me] = source
        scatter_to(size - 1, to, lambda k: ref.at[me], ref.at[me], wsend.at[phase, count], wrecv.at[phase, count])

    def gain_sum(phase, size, ref):
        whole(ref.at[pl.ds(0, size - 1)], wrecv.at[phase, count])
        return added(ref, size)

    def during(l):
        for step in DURING.get(layers - 1 - l, ()):
            advance(step)

    whole(fetched.at[0], recv_sem.at[1])
    forward(0)
    g0[0] = jnp.zeros_like(g0[0])
    backward(0, lambda l: None)
    line_up(0)
    send_back(0)
    whole(fetched.at[1], recv_sem.at[2])
    forward(1)
    backward(1, during)

    gain_pair = remote(g0.at[0], g0.at[1], wsend.at[0, count], wrecv.at[0, count], sibling)
    gain_pair.start()
    line_up(1)
    advance((layers - 1, 1))
    gain_pair.wait_recv()
    gain_axis(1, x, x_size, x_device, g0[0] + g0[1], g1)
    along(1)
    rounds = 2 * y_size
    send_back(1, (0, rounds // 2))
    along(0)
    told(1)
    gain_axis(2, y, y_size, y_device, gain_sum(1, x_size, g1), g2)
    send_back(1, (rounds // 2, rounds * 3 // 4))
    whole(returned.at[0], recv_sem.at[3])
    conv[0:rows, :] = dot(add[0], returned[0])
    told(0)
    send_back(1, (rounds * 3 // 4, rounds))
    gain_axis(3, z, z_size, z_device, gain_sum(2, y_size, g2), g3)
    across_back(1)
    across_back(0)

    share = rows // x_size
    whole(returned.at[1], recv_sem.at[4])
    tsend[...] = (conv[0:rows, :] + dot(add[1], returned[1])).astype(BF16).reshape(x_size, share, width)
    pltpu.make_async_copy(tsend.at[x], trecv.at[x], recv_sem.at[5]).start()
    scatter_to(x_size - 1, x_device, lambda k: tsend.at[x_index(k)], trecv.at[x], send_sem.at[5], recv_sem.at[5])
    pair_back(1)
    whole(trecv, recv_sem.at[5])
    table_out[x] = added(trecv, x_size).astype(BF16)
    scatter_to(x_size - 1, x_device, lambda k: table_out.at[x], table_out.at[x], send_sem.at[6], recv_sem.at[6])

    pair_back(0)
    gain_out[...] = gain_sum(3, z_size, g3)
    for h in range(2):
        whole(weight_out.at[pl.ds(h * deep, deep), theirs], wrecv.at[4, h])
    whole(table_out.at[pl.ds(0, x_size - 1)], recv_sem.at[6])

    whole(ask.at[pl.ds(0, shards - 1)], send_sem.at[0])
    for m in range(MB):
        if m:
            whole(serve.at[m, pl.ds(0, slots - CAP)], send_sem.at[1 + m])
        whole(back.at[m, pl.ds(0, slots - CAP)], send_sem.at[3 + m])
    whole(tsend.at[pl.ds(0, x_size - 1)], send_sem.at[5])
    whole(tsend.at[pl.ds(0, x_size - 1)], send_sem.at[6])
    for b in range(count):
        whole(s0.at[of(b)], wsend.at[0, b])
        whole(r1[b].at[pl.ds(0, plane - 1)], wsend.at[1, b])
    for h in range(2):
        for _ in range(deep):
            whole(r1[0].at[pl.ds(0, plane - 1)], wsend.at[3, h])
        whole(weight_out.at[pl.ds(h * deep, deep), ours], wsend.at[4, h])
        whole(s2[h].at[pl.ds(0, z_size - 1)], wsend.at[2, h])
        whole(t2[h].at[pl.ds(0, z_size - 1)], wsend.at[5, h])
    gain_pair.wait_send()
    whole(g1.at[pl.ds(0, x_size - 1)], wsend.at[1, count])
    whole(g2.at[pl.ds(0, y_size - 1)], wsend.at[2, count])
    whole(g3.at[pl.ds(0, z_size - 1)], wsend.at[3, count])


def scale_kernel(scale, weight_ref, gain_ref, table_ref, weight_out, gain_out, table_out,
                 weight, wide, table, tall, load_sem, store_sem):
    layers = weight.shape[0]
    loads = [pltpu.make_async_copy(weight_ref.at[l], weight.at[l], load_sem.at[l]) for l in range(layers)]
    loads.append(pltpu.make_async_copy(table_ref, table, load_sem.at[layers]))
    stores = [pltpu.make_async_copy(wide.at[l], weight_out.at[l], store_sem.at[l]) for l in range(layers)]
    stores.append(pltpu.make_async_copy(tall, table_out, store_sem.at[layers]))
    for load in loads:
        load.start()
    gain_out[...] = gain_ref[...] * scale
    for l in range(layers):
        loads[l].wait()
        wide[l] = weight[l].astype(F32) * scale
        stores[l].start()
    loads[layers].wait()
    tall[...] = table[...].astype(F32)
    stores[layers].start()
    for store in stores:
        store.wait()


def body(table, owner, row, conv_weight, gain, upstream):
    shards, seq_axis = lax.axis_size("emb"), lax.axis_size("seq")
    _, tokens = row.shape
    rows, width = table.shape
    layers, taps, _ = conv_weight.shape
    slots = shards * CAP
    z_size, y_size, _, x_size = plan(shards, seq_axis)
    sets = batches_of(layers)
    shape = jax.ShapeDtypeStruct
    dma = pltpu.SemaphoreType.DMA
    half = taps // 2
    share = rows // x_size
    plane = x_size * y_size
    high = half // (plane // 2)
    one_z = (z_size, -(-(layers // 2) * high // z_size // 16) * 16, LANES)
    shapes = [(plane, n, high, LANES) for _, n in sets] + [(layers // 2, high, LANES)] * 2 + [one_z] * 6
    work = [pltpu.VMEM(dims, BF16) for dims in shapes]
    near = pl.BlockSpec(memory_space=pltpu.VMEM)
    far = pl.BlockSpec(memory_space=pl.ANY)
    weight_sum, gain_sum, table_grad = pl.pallas_call(
        functools.partial(window_kernel, shards, seq_axis, 64),
        out_shape=[
            shape((layers, taps, width), BF16),
            shape((layers, width), F32),
            shape((x_size, share, width), BF16),
        ],
        in_specs=[near, near, near, near, far, far],
        out_specs=[near, near, near],
        scratch_shapes=[
            pltpu.VMEM((shards, MB, LANES), I32),
            pltpu.VMEM((shards, MB, LANES), I32),
            pltpu.VMEM((MB, slots, width), BF16),
            pltpu.VMEM((MB, slots, width), BF16),
            pltpu.VMEM((MB, slots, width), BF16),
            pltpu.VMEM((MB, slots, width), BF16),
            pltpu.VMEM((MB, tokens, slots), BF16),
            pltpu.VMEM((MB, slots, tokens), BF16),
            pltpu.VMEM((MB, rows, slots), BF16),
            pltpu.VMEM((layers, taps, width), F32),
            pltpu.VMEM((MB, tokens, width), BF16),
            pltpu.VMEM((layers, taps, width), BF16),
            pltpu.VMEM((tokens + 32, width), F32),
            pltpu.VMEM((max(tokens, rows), width), F32),
            pltpu.VMEM((MB, layers, tokens, width), F32),
            pltpu.VMEM((MB, layers, tokens, LANES), F32),
            pltpu.VMEM((MB, layers, tokens, width), F32),
            pltpu.VMEM((MB, layers, tokens, taps), BF16),
            pltpu.VMEM((MB, tokens, taps), BF16),
            pltpu.VMEM((MB, tokens, width), BF16),
            pltpu.VMEM((layers, taps, width), F32),
            pltpu.VMEM((x_size, share, width), BF16),
            pltpu.VMEM((x_size, share, width), BF16),
            pltpu.VMEM((layers, half, width), BF16),
            pltpu.VMEM((layers, half, width), BF16),
            pltpu.VMEM((layers, half, width), BF16),
            pltpu.VMEM((2, layers, width), F32),
            pltpu.VMEM((x_size, layers, width), F32),
            pltpu.VMEM((y_size, layers, width), F32),
            pltpu.VMEM((z_size, layers, width), F32),
            dma((2,)),
            dma((7,)),
            dma((7,)),
            dma((6, len(sets) + 1)),
            dma((6, len(sets) + 1)),
            *work,
        ],
        compiler_params=pltpu.CompilerParams(
            collective_id=0, has_side_effects=True, vmem_limit_bytes=60 * 2**20
        ),
    )(owner.reshape(MB, 1, tokens), row, table, gain, conv_weight, upstream)
    scale = float(MB * tokens * shards * seq_axis) ** (-0.5)
    return pl.pallas_call(
        functools.partial(scale_kernel, scale),
        out_shape=[shape((layers, taps, width), F32), shape((layers, width), F32), shape((rows, width), F32)],
        in_specs=[far, near, far],
        out_specs=[far, near, far],
        scratch_shapes=[
            pltpu.VMEM((layers, taps, width), BF16),
            pltpu.VMEM((layers, taps, width), F32),
            pltpu.VMEM((rows, width), BF16),
            pltpu.VMEM((rows, width), F32),
            dma((layers + 1,)),
            dma((layers + 1,)),
        ],
        compiler_params=pltpu.CompilerParams(vmem_limit_bytes=60 * 2**20),
    )(weight_sum, gain_sum, table_grad.reshape(rows, width))


def solution(mesh):
    in_specs = (
        P("emb", None),
        P(("emb", "seq"), None, None),
        P(("emb", "seq"), None),
        P(),
        P(),
        P(("emb", "seq"), None, None),
    )
    out_specs = (P(), P(), P("emb", None))
    return jax.shard_map(body, mesh=mesh, in_specs=in_specs, out_specs=out_specs, check_vma=False)
```

```python
import functools
import math

import jax
import jax.numpy as jnp
from jax import lax
from jax.experimental import pallas as pl
from jax.experimental.pallas import tpu as pltpu
from jax.sharding import PartitionSpec as P

MB = 2
CAP = 16
LANES = 128
F32 = jnp.float32
BF16 = jnp.bfloat16
I32 = jnp.int32
NT = (((1,), (1,)), ((), ()))
TN = (((0,), (0,)), ((), ()))


def plan(shards, seq_axis):
    core = 2
    y = 4 if shards >= 64 else 2
    return shards // (core * y), y, core, seq_axis


def iota(shape, axis):
    return lax.broadcasted_iota(I32, shape, axis)


def dot(a, b, dims=(((1,), (0,)), ((), ()))):
    return lax.dot_general(a, b, dims, preferred_element_type=F32)


def whole(ref, sem):
    pltpu.make_async_copy(ref, ref, sem).wait()


def greet(peers):
    barrier = pltpu.get_barrier_semaphore()
    total = 0
    for count, device in peers:

        def hello(k, carry, device=device):
            pl.semaphore_signal(barrier, inc=1, device_id=device(k), device_id_type=pl.DeviceIdType.MESH)
            return carry

        lax.fori_loop(0, count, hello, 0)
        total += count
    return total


def scatter_to(count, device, src, dst, send_sem, recv_sem):
    def step(k, carry):
        pltpu.make_async_remote_copy(
            src_ref=src(k),
            dst_ref=dst,
            send_sem=send_sem,
            recv_sem=recv_sem,
            device_id=device(k),
            device_id_type=pl.DeviceIdType.MESH,
        ).start()
        return carry

    lax.fori_loop(0, count, step, 0)


def emb_peer(shards):
    me, x = lax.axis_index("emb"), lax.axis_index("seq")

    def index(k):
        return lax.rem(me + k + 1, shards)

    return index, lambda k: (index(k), x)


def to_emb(sizes, src, dst, send_sem, recv_sem, rounds=None):
    z_size, y_size, core, _ = sizes
    line = y_size * core
    me, x = lax.axis_index("emb"), lax.axis_index("seq")
    c, y, z = lax.rem(me, core), lax.rem(me // core, y_size), me // line
    steps = sorted(range(-((z_size - 1) // 2), z_size // 2 + 1), key=lambda d: (-abs(d), -d))
    levels = [lax.rem(z + d + z_size, z_size) * line for d in steps]

    def send(level, near):
        peer = level + near
        pltpu.make_async_remote_copy(
            src_ref=src(peer),
            dst_ref=dst,
            send_sem=send_sem,
            recv_sem=recv_sem,
            device_id=(peer, x),
            device_id_type=pl.DeviceIdType.MESH,
        ).start()

    def step(j, carry):
        k = line - 1 - j
        near = lax.rem(y + k // core, y_size) * core + lax.rem(c + k, core)
        for level in levels:
            send(level, near)
        return carry

    first, last = rounds or (0, line)
    lax.fori_loop(first, min(last, line - 1), step, 0)
    if last == line:
        for level in levels[:-1]:
            send(level, y * core + c)


def requests(owner, row, shards, lane0):
    tokens = owner.shape[1]
    named = iota((shards, tokens), 0) == owner
    marks = jnp.where(named, 1.0, 0.0).astype(F32)
    upto = jnp.where(iota((tokens, tokens), 0) <= iota((tokens, tokens), 1), 1.0, 0.0).astype(BF16)
    ranks = dot(marks.astype(BF16), upto)
    slot = jnp.sum(marks * ranks, axis=0, keepdims=True).astype(I32) - 1
    high = (row // 16).astype(F32)
    low = (row % 16).astype(F32)
    values = jnp.concatenate([marks * high, marks * low], axis=0).astype(BF16)
    places = jnp.where(iota((LANES, tokens), 0) == slot + lane0, 1.0, 0.0).astype(BF16)
    wanted = dot(values, places, NT)
    wanted = wanted[:shards] * 16.0 + wanted[shards:]
    return owner * CAP + slot, wanted.astype(I32)


DURING = {0: [(0, 0)], 1: [(0, 1), (1, 0)], 2: [(1, 1), (2, 0)], 3: [(2, 1), (3, 0)]}


def batches_of(layers):
    return [(l, 1) for l in reversed(range(layers))]


def window_kernel(shards, seq_axis, chunk,
                  owner_ref, row_ref, table_ref, gain_ref, weight_hbm, up_hbm,
                  weight_out, gain_out, table_out,
                  ask, asked, serve, fetched, back, returned, pick, place, add,
                  weight_ref, up_ref, wide, padded, conv, normed, inverse, slope, hidden, dwide, grad_ref,
                  dweight_ref, tsend, trecv, s0, r0, s1, g0, g1, g2, g3,
                  load_sem, send_sem, recv_sem, wsend, wrecv, *work):
    sizes = plan(shards, seq_axis)
    z_size, y_size, _, x_size = sizes
    layers, taps, width = weight_ref.shape
    tokens = row_ref.shape[1]
    rows = table_ref.shape[0]
    slots = shards * CAP
    groups = shards // 8
    e, x = lax.axis_index("emb"), lax.axis_index("seq")
    c = lax.rem(e, 2)
    y = lax.rem(e // 2, y_size)
    z = e // (2 * y_size)
    _, device = emb_peer(shards)
    sibling = (e + 1 - 2 * c, x)
    half = taps // 2
    sets = batches_of(layers)
    count = len(sets)
    r1 = work[:count]
    r3, s2, r2, t2 = (work[count + 2 * k : count + 2 * k + 2] for k in range(4))
    plane = x_size * y_size
    p_me = x * y_size + y
    high = half // (plane // 2)

    def x_index(k):
        return lax.rem(x + k + 1, x_size)

    def x_device(k):
        return (e, x_index(k))

    def y_index(k):
        return lax.rem(y + k + 1, y_size)

    def y_device(k):
        return ((z * y_size + y_index(k)) * 2 + c, x)

    def p_index(k):
        return lax.rem(p_me + k + 1, plane)

    def p_device(k):
        p = p_index(k)
        return ((z * y_size + lax.rem(p, y_size)) * 2 + c, p // y_size)

    def off_device(k):
        py = lax.rem(y + 1 + lax.rem(k, y_size - 1), y_size)
        px = lax.rem(x + 1 + k // (y_size - 1), x_size)
        return ((z * y_size + py) * 2 + c, px)

    def z_index(k):
        return lax.rem(z + k + 1, z_size)

    def z_device(k):
        return ((z_index(k) * y_size + y) * 2 + c, x)

    def remote(src, dst, send, recv, to):
        return pltpu.make_async_remote_copy(
            src_ref=src, dst_ref=dst, send_sem=send, recv_sem=recv, device_id=to, device_id_type=pl.DeviceIdType.MESH
        )

    load_weight = pltpu.make_async_copy(weight_hbm, weight_ref, load_sem.at[0])
    load_up = pltpu.make_async_copy(up_hbm, up_ref, load_sem.at[1])
    load_weight.start()
    load_up.start()
    expected = greet([(shards - 1, device), (x_size - 1, x_device), ((x_size - 1) * (y_size - 1), off_device)])

    lane0 = lax.rem(e, 8) * CAP
    places = []
    for m in range(MB):
        q, wanted = requests(owner_ref[m], row_ref[m : m + 1, :], shards, lane0)
        ask[:, m, :] = wanted
        places.append(q)
    pl.semaphore_wait(pltpu.get_barrier_semaphore(), expected)
    pltpu.make_async_copy(ask.at[e], asked.at[e], recv_sem.at[0]).start()
    to_emb(sizes, lambda peer: ask.at[peer], asked.at[e], send_sem.at[0], recv_sem.at[0])

    for m in range(MB):
        column = jnp.broadcast_to(places[m].astype(F32), (LANES, tokens)).T
        for s in range(0, slots, LANES):
            pick[m, :, s : s + LANES] = jnp.where(
                column == (iota((tokens, LANES), 1) + s).astype(F32), 1.0, 0.0
            ).astype(BF16)
            place[m, s : s + LANES, :] = jnp.where(iota((LANES, tokens), 0) + s == places[m], 1.0, 0.0).astype(BF16)
    load_weight.wait()
    for l in range(layers):
        wide[l] = weight_ref[l].astype(BF16)
    pad = (padded.shape[0] - tokens) // 2
    padded[0:pad, :] = jnp.zeros((pad, width), F32)
    padded[pad + tokens :, :] = jnp.zeros((pad, width), F32)

    here = pl.ds(pl.multiple_of(e * CAP, CAP), CAP)
    whole(asked, recv_sem.at[0])
    wanted = []
    for m in range(MB):
        ids = jnp.sum(asked[:, m, :].reshape(groups, 8, LANES), axis=1)
        wanted.append(ids)
        tall = jnp.concatenate([ids.astype(F32)] * (LANES // groups), axis=0).T
        for g in range(groups):
            hot = jnp.where(iota((LANES, rows), 1).astype(F32) == tall[:, g : g + 1], 1.0, 0.0).astype(BF16)
            serve[m, g * LANES : (g + 1) * LANES, :] = dot(hot, table_ref[...]).astype(BF16)
        if m:
            whole(serve.at[0, pl.ds(0, slots - CAP)], send_sem.at[1])
        pltpu.make_async_copy(serve.at[m, here], fetched.at[m, here], recv_sem.at[1 + m]).start()
        to_emb(
            sizes,
            lambda peer, m=m: serve.at[m, pl.ds(pl.multiple_of(peer * CAP, CAP), CAP)],
            fetched.at[m, here],
            send_sem.at[1 + m],
            recv_sem.at[1 + m],
        )
    for m in range(MB):
        for g in range(groups):
            add[m, :, g * LANES : (g + 1) * LANES] = jnp.where(
                iota((rows, LANES), 0) == wanted[m][g : g + 1, :], 1.0, 0.0
            ).astype(BF16)
    load_up.wait()

    spans = [slice(at, at + chunk) for at in range(0, tokens, chunk)]
    inv_width = 1.0 / width
    k0 = math.sqrt(2.0 / math.pi)

    def forward(m):
        conv[...] = dot(pick[m], fetched[m])
        for l in range(layers):
            d = 2**l
            gain = gain_ref[l : l + 1, :]
            for at in spans:
                if l == 0:
                    state = conv[at, :]
                else:
                    state = normed[m, l, at, :]
                centred = state - jnp.sum(state, axis=-1, keepdims=True) * inv_width
                rstd = lax.rsqrt(jnp.sum(centred * centred, axis=-1, keepdims=True) * inv_width + 1e-05)
                norm = centred * rstd
                if l < layers - 1:
                    normed[m, l + 1, at, :] = state
                normed[m, l, at, :] = norm
                inverse[m, l, at, :] = jnp.broadcast_to(rstd, (chunk, LANES))
                padded[pad + at.start : pad + at.stop, :] = norm * gain
            for k in range(3):
                for at in spans:
                    moved = padded[pad + at.start - k * d : pad + at.stop - k * d, :]
                    hidden[m, l, at, k * width : (k + 1) * width] = moved.astype(BF16)
            conv[...] = dot(hidden[m, l], wide[l])
            for at in spans:
                v = conv[at, :]
                v2 = v * v
                t = jnp.tanh(v * (k0 + (k0 * 0.044715) * v2))
                side = 0.5 + 0.5 * t
                slope[m, l, at, :] = side + v * (0.5 - 0.5 * t * t) * (k0 + (3 * k0 * 0.044715) * v2)
                if l < layers - 1:
                    state = normed[m, l + 1, at, :]
                    normed[m, l + 1, at, :] = (state + v * side).astype(BF16).astype(F32)

    def backward(m, after):
        for l in reversed(range(layers)):
            d = 2**l
            gain = gain_ref[l : l + 1, :]
            src = up_ref if l == layers - 1 else grad_ref
            for at in spans:
                padded[pad + at.start : pad + at.stop, :] = src[m, at, :].astype(F32) * slope[m, l, at, :]
            for k in range(3):
                for at in spans:
                    moved = padded[pad + at.start + k * d : pad + at.stop + k * d, :]
                    dwide[m, at, k * width : (k + 1) * width] = moved.astype(BF16)
            for k in range(3):
                part = dot(hidden[m, l, :, 0:width], dwide[m, :, k * width : (k + 1) * width], TN)
                taken = slice(k * width, (k + 1) * width)
                if m == 0:
                    dweight_ref[l, taken, :] = part
                else:
                    dweight_ref[l, taken, :] += part
            dh = dot(dwide[m, :, 0:width], wide[l, 0:width, :], NT)
            dh = dh + dot(dwide[m, :, width : 2 * width], wide[l, width : 2 * width, :], NT)
            dh = dh + dot(dwide[m, :, 2 * width :], wide[l, 2 * width :, :], NT)
            conv[...] = dh
            dgain = jnp.zeros((1, width), F32)
            for at in spans:
                dh = conv[at, :]
                norm = normed[m, l, at, :]
                both = dh * norm
                dgain = dgain + jnp.sum(both, axis=0, keepdims=True)
                dn = dh * gain
                m1 = jnp.sum(dn, axis=-1, keepdims=True) * inv_width
                m2 = jnp.sum(both * gain, axis=-1, keepdims=True) * inv_width
                rstd = inverse[m, l, at, 0:1]
                grad_ref[m, at, :] = (
                    src[m, at, :].astype(F32) + rstd * (dn - m1 - norm * m2)
                ).astype(BF16)
            if m == 0:
                g0[0, l : l + 1, :] = dgain
            else:
                g0[0, l : l + 1, :] += dgain
            after(l)

    def line_up(m):
        for s in range(0, slots, LANES):
            back[m, s : s + LANES, :] = dot(place[m, s : s + LANES, :], grad_ref[m]).astype(BF16)
        pltpu.make_async_copy(back.at[m, here], returned.at[m, here], recv_sem.at[3 + m]).start()

    def send_back(m, rounds=None):
        to_emb(
            sizes,
            lambda peer: back.at[m, pl.ds(pl.multiple_of(peer * CAP, CAP), CAP)],
            returned.at[m, here],
            send_sem.at[3 + m],
            recv_sem.at[3 + m],
            rounds,
        )

    theirs = pl.ds(pl.multiple_of((1 - c) * half, half), half)
    ours = pl.ds(pl.multiple_of(c * half, half), half)


    def of(b):
        return pl.ds(sets[b][0], sets[b][1])

    def piece(some, p, start):
        return (
            some,
            pl.ds(pl.multiple_of(start + (p // 2) * high, 16), high),
            pl.ds(pl.multiple_of(lax.rem(p, 2) * LANES, LANES), LANES),
        )

    def added(ref, size):
        total = ref[0].astype(F32)
        for k in range(1, size):
            total = total + ref[k].astype(F32)
        return total

    def pair(b):
        for l in range(sets[b][0], sum(sets[b])):
            s0[l] = dweight_ref[l, theirs, :].astype(BF16)
        remote(s0.at[of(b)], r0.at[of(b)], wsend.at[0, b], wrecv.at[0, b], sibling).start()

    def across(b):
        whole(r0.at[of(b)], wrecv.at[0, b])
        for l in range(sets[b][0], sum(sets[b])):
            s1[l] = (dweight_ref[l, ours, :] + r0[l].astype(F32)).astype(BF16)
        pltpu.make_async_copy(s1.at[piece(of(b), p_me, 0)], r1[b].at[p_me], wrecv.at[1, b]).start()
        scatter_to(
            plane - 1, p_device, lambda k: s1.at[piece(of(b), p_index(k), 0)], r1[b].at[p_me], wsend.at[1, b], wrecv.at[1, b]
        )

    deep = layers // 2
    per_z = deep * high // z_size

    def along(h):
        parts = []
        for l in range(h * deep, (h + 1) * deep):
            b = layers - 1 - l
            whole(r1[b], wrecv.at[1, b])
            parts.append(added(r1[b], plane).reshape(high, LANES))
        total = jnp.concatenate(parts, axis=0)
        for k in range(z_size):
            s2[h][k, 0:per_z, :] = total[k * per_z : (k + 1) * per_z].astype(BF16)
        pltpu.make_async_copy(s2[h].at[z], r2[h].at[z], wrecv.at[2, h]).start()
        scatter_to(z_size - 1, z_device, lambda k: s2[h].at[z_index(k)], r2[h].at[z], wsend.at[2, h], wrecv.at[2, h])

    def told(h):
        whole(r2[h], wrecv.at[2, h])
        t2[h][z] = added(r2[h], z_size).astype(BF16)
        scatter_to(z_size - 1, z_device, lambda k: t2[h].at[z], t2[h].at[z], wsend.at[5, h], wrecv.at[5, h])

    def across_back(h):
        whole(t2[h].at[pl.ds(0, z_size - 1)], wrecv.at[5, h])
        total = jnp.concatenate([t2[h][k, 0:per_z, :].astype(F32) for k in range(z_size)], axis=0)
        r3[h][...] = total.reshape(deep, high, LANES).astype(BF16)
        spot = weight_out.at[piece(pl.ds(h * deep, deep), p_me, c * half)]
        pltpu.make_async_copy(r3[h], spot, wrecv.at[3, h]).start()
        scatter_to(plane - 1, p_device, lambda k: r3[h], spot, wsend.at[3, h], wrecv.at[3, h])

    def pair_back(h):
        done = weight_out.at[pl.ds(h * deep, deep), ours]
        whole(done, wrecv.at[3, h])
        remote(done, done, wsend.at[4, h], wrecv.at[4, h], sibling).start()

    way = [pair, across]

    def advance(*steps):
        for b, phase in steps:
            way[phase](b)

    def gain_axis(phase, me, size, to, source, ref):
        ref[me] = source
        scatter_to(size - 1, to, lambda k: ref.at[me], ref.at[me], wsend.at[phase, count], wrecv.at[phase, count])

    def gain_sum(phase, size, ref):
        whole(ref.at[pl.ds(0, size - 1)], wrecv.at[phase, count])
        return added(ref, size)

    def during(l):
        for step in DURING.get(layers - 1 - l, ()):
            advance(step)

    whole(fetched.at[0], recv_sem.at[1])
    forward(0)
    g0[0] = jnp.zeros_like(g0[0])
    backward(0, lambda l: None)
    line_up(0)
    send_back(0)
    whole(fetched.at[1], recv_sem.at[2])
    forward(1)
    backward(1, during)

    gain_pair = remote(g0.at[0], g0.at[1], wsend.at[0, count], wrecv.at[0, count], sibling)
    gain_pair.start()
    line_up(1)
    advance((layers - 1, 1))
    gain_pair.wait_recv()
    gain_axis(1, x, x_size, x_device, g0[0] + g0[1], g1)
    along(1)
    rounds = 2 * y_size
    send_back(1, (0, rounds // 2))
    along(0)
    told(1)
    gain_axis(2, y, y_size, y_device, gain_sum(1, x_size, g1), g2)
    send_back(1, (rounds // 2, rounds * 3 // 4))
    whole(returned.at[0], recv_sem.at[3])
    conv[0:rows, :] = dot(add[0], returned[0])
    told(0)
    send_back(1, (rounds * 3 // 4, rounds))
    gain_axis(3, z, z_size, z_device, gain_sum(2, y_size, g2), g3)
    across_back(1)
    across_back(0)

    share = rows // x_size
    whole(returned.at[1], recv_sem.at[4])
    tsend[...] = (conv[0:rows, :] + dot(add[1], returned[1])).astype(BF16).reshape(x_size, share, width)
    pltpu.make_async_copy(tsend.at[x], trecv.at[x], recv_sem.at[5]).start()
    scatter_to(x_size - 1, x_device, lambda k: tsend.at[x_index(k)], trecv.at[x], send_sem.at[5], recv_sem.at[5])
    pair_back(1)
    whole(trecv, recv_sem.at[5])
    table_out[x] = added(trecv, x_size).astype(BF16)
    scatter_to(x_size - 1, x_device, lambda k: table_out.at[x], table_out.at[x], send_sem.at[6], recv_sem.at[6])

    pair_back(0)
    gain_out[...] = gain_sum(3, z_size, g3)
    for h in range(2):
        whole(weight_out.at[pl.ds(h * deep, deep), theirs], wrecv.at[4, h])
    whole(table_out.at[pl.ds(0, x_size - 1)], recv_sem.at[6])

    whole(ask.at[pl.ds(0, shards - 1)], send_sem.at[0])
    for m in range(MB):
        if m:
            whole(serve.at[m, pl.ds(0, slots - CAP)], send_sem.at[1 + m])
        whole(back.at[m, pl.ds(0, slots - CAP)], send_sem.at[3 + m])
    whole(tsend.at[pl.ds(0, x_size - 1)], send_sem.at[5])
    whole(tsend.at[pl.ds(0, x_size - 1)], send_sem.at[6])
    for b in range(count):
        whole(s0.at[of(b)], wsend.at[0, b])
        whole(r1[b].at[pl.ds(0, plane - 1)], wsend.at[1, b])
    for h in range(2):
        for _ in range(deep):
            whole(r1[0].at[pl.ds(0, plane - 1)], wsend.at[3, h])
        whole(weight_out.at[pl.ds(h * deep, deep), ours], wsend.at[4, h])
        whole(s2[h].at[pl.ds(0, z_size - 1)], wsend.at[2, h])
        whole(t2[h].at[pl.ds(0, z_size - 1)], wsend.at[5, h])
    gain_pair.wait_send()
    whole(g1.at[pl.ds(0, x_size - 1)], wsend.at[1, count])
    whole(g2.at[pl.ds(0, y_size - 1)], wsend.at[2, count])
    whole(g3.at[pl.ds(0, z_size - 1)], wsend.at[3, count])


def scale_kernel(scale, weight_ref, gain_ref, table_ref, weight_out, gain_out, table_out):
    weight_out[...] = weight_ref[...].astype(F32) * scale
    gain_out[...] = gain_ref[...] * scale
    table_out[...] = table_ref[...].astype(F32)


def body(table, owner, row, conv_weight, gain, upstream):
    shards, seq_axis = lax.axis_size("emb"), lax.axis_size("seq")
    _, tokens = row.shape
    rows, width = table.shape
    layers, taps, _ = conv_weight.shape
    slots = shards * CAP
    z_size, y_size, _, x_size = plan(shards, seq_axis)
    sets = batches_of(layers)
    shape = jax.ShapeDtypeStruct
    dma = pltpu.SemaphoreType.DMA
    half = taps // 2
    share = rows // x_size
    plane = x_size * y_size
    high = half // (plane // 2)
    one_z = (z_size, -(-(layers // 2) * high // z_size // 16) * 16, LANES)
    shapes = [(plane, n, high, LANES) for _, n in sets] + [(layers // 2, high, LANES)] * 2 + [one_z] * 6
    work = [pltpu.VMEM(dims, BF16) for dims in shapes]
    near = pl.BlockSpec(memory_space=pltpu.VMEM)
    far = pl.BlockSpec(memory_space=pl.ANY)
    weight_sum, gain_sum, table_grad = pl.pallas_call(
        functools.partial(window_kernel, shards, seq_axis, 64),
        out_shape=[
            shape((layers, taps, width), BF16),
            shape((layers, width), F32),
            shape((x_size, share, width), BF16),
        ],
        in_specs=[near, near, near, near, far, far],
        out_specs=[near, near, near],
        scratch_shapes=[
            pltpu.VMEM((shards, MB, LANES), I32),
            pltpu.VMEM((shards, MB, LANES), I32),
            pltpu.VMEM((MB, slots, width), BF16),
            pltpu.VMEM((MB, slots, width), BF16),
            pltpu.VMEM((MB, slots, width), BF16),
            pltpu.VMEM((MB, slots, width), BF16),
            pltpu.VMEM((MB, tokens, slots), BF16),
            pltpu.VMEM((MB, slots, tokens), BF16),
            pltpu.VMEM((MB, rows, slots), BF16),
            pltpu.VMEM((layers, taps, width), F32),
            pltpu.VMEM((MB, tokens, width), BF16),
            pltpu.VMEM((layers, taps, width), BF16),
            pltpu.VMEM((tokens + 32, width), F32),
            pltpu.VMEM((max(tokens, rows), width), F32),
            pltpu.VMEM((MB, layers, tokens, width), F32),
            pltpu.VMEM((MB, layers, tokens, LANES), F32),
            pltpu.VMEM((MB, layers, tokens, width), F32),
            pltpu.VMEM((MB, layers, tokens, taps), BF16),
            pltpu.VMEM((MB, tokens, taps), BF16),
            pltpu.VMEM((MB, tokens, width), BF16),
            pltpu.VMEM((layers, taps, width), F32),
            pltpu.VMEM((x_size, share, width), BF16),
            pltpu.VMEM((x_size, share, width), BF16),
            pltpu.VMEM((layers, half, width), BF16),
            pltpu.VMEM((layers, half, width), BF16),
            pltpu.VMEM((layers, half, width), BF16),
            pltpu.VMEM((2, layers, width), F32),
            pltpu.VMEM((x_size, layers, width), F32),
            pltpu.VMEM((y_size, layers, width), F32),
            pltpu.VMEM((z_size, layers, width), F32),
            dma((2,)),
            dma((7,)),
            dma((7,)),
            dma((6, len(sets) + 1)),
            dma((6, len(sets) + 1)),
            *work,
        ],
        compiler_params=pltpu.CompilerParams(
            collective_id=0, has_side_effects=True, vmem_limit_bytes=60 * 2**20
        ),
    )(owner.reshape(MB, 1, tokens), row, table, gain, conv_weight, upstream)
    scale = float(MB * tokens * shards * seq_axis) ** (-0.5)
    halves = [
        pl.BlockSpec((layers // 2, taps, width), lambda k: (k, 0, 0)),
        pl.BlockSpec((layers, width), lambda k: (0, 0)),
        pl.BlockSpec((rows // 2, width), lambda k: (k, 0)),
    ]
    return pl.pallas_call(
        functools.partial(scale_kernel, scale),
        grid=(2,),
        out_shape=[shape((layers, taps, width), F32), shape((layers, width), F32), shape((rows, width), F32)],
        in_specs=halves,
        out_specs=halves,
        compiler_params=pltpu.CompilerParams(vmem_limit_bytes=60 * 2**20),
    )(weight_sum, gain_sum, table_grad.reshape(rows, width))


def solution(mesh):
    in_specs = (
        P("emb", None),
        P(("emb", "seq"), None, None),
        P(("emb", "seq"), None),
        P(),
        P(),
        P(("emb", "seq"), None, None),
    )
    out_specs = (P(), P(), P("emb", None))
    return jax.shard_map(body, mesh=mesh, in_specs=in_specs, out_specs=out_specs, check_vma=False)
```

```python
import functools
import math

import jax
import jax.numpy as jnp
from jax import lax
from jax.experimental import pallas as pl
from jax.experimental.pallas import tpu as pltpu
from jax.sharding import PartitionSpec as P

MB = 2
CAP = 16
LANES = 128
F32 = jnp.float32
BF16 = jnp.bfloat16
I32 = jnp.int32
NT = (((1,), (1,)), ((), ()))
TN = (((0,), (0,)), ((), ()))


def plan(shards, seq_axis):
    core = 2
    y = 4 if shards >= 64 else 2
    return shards // (core * y), y, core, seq_axis


def iota(shape, axis):
    return lax.broadcasted_iota(I32, shape, axis)


def dot(a, b, dims=(((1,), (0,)), ((), ()))):
    return lax.dot_general(a, b, dims, preferred_element_type=F32)


def whole(ref, sem):
    pltpu.make_async_copy(ref, ref, sem).wait()


def greet(peers):
    barrier = pltpu.get_barrier_semaphore()
    total = 0
    for count, device in peers:

        def hello(k, carry, device=device):
            pl.semaphore_signal(barrier, inc=1, device_id=device(k), device_id_type=pl.DeviceIdType.MESH)
            return carry

        lax.fori_loop(0, count, hello, 0)
        total += count
    return total


def scatter_to(count, device, src, dst, send_sem, recv_sem):
    def step(k, carry):
        pltpu.make_async_remote_copy(
            src_ref=src(k),
            dst_ref=dst,
            send_sem=send_sem,
            recv_sem=recv_sem,
            device_id=device(k),
            device_id_type=pl.DeviceIdType.MESH,
        ).start()
        return carry

    lax.fori_loop(0, count, step, 0)


def emb_peer(shards):
    me, x = lax.axis_index("emb"), lax.axis_index("seq")

    def index(k):
        return lax.rem(me + k + 1, shards)

    return index, lambda k: (index(k), x)


def to_emb(sizes, src, dst, send_sem, recv_sem, rounds=None):
    z_size, y_size, core, _ = sizes
    line = y_size * core
    me, x = lax.axis_index("emb"), lax.axis_index("seq")
    c, y, z = lax.rem(me, core), lax.rem(me // core, y_size), me // line
    steps = sorted(range(-((z_size - 1) // 2), z_size // 2 + 1), key=lambda d: (-abs(d), -d))
    levels = [lax.rem(z + d + z_size, z_size) * line for d in steps]

    def send(level, near):
        peer = level + near
        pltpu.make_async_remote_copy(
            src_ref=src(peer),
            dst_ref=dst,
            send_sem=send_sem,
            recv_sem=recv_sem,
            device_id=(peer, x),
            device_id_type=pl.DeviceIdType.MESH,
        ).start()

    def step(j, carry):
        k = line - 1 - j
        near = lax.rem(y + k // core, y_size) * core + lax.rem(c + k, core)
        for level in levels:
            send(level, near)
        return carry

    first, last = rounds or (0, line)
    lax.fori_loop(first, min(last, line - 1), step, 0)
    if last == line:
        for level in levels[:-1]:
            send(level, y * core + c)


def requests(owner, row, shards, lane0):
    tokens = owner.shape[1]
    named = iota((shards, tokens), 0) == owner
    marks = jnp.where(named, 1.0, 0.0).astype(F32)
    upto = jnp.where(iota((tokens, tokens), 0) <= iota((tokens, tokens), 1), 1.0, 0.0).astype(BF16)
    ranks = dot(marks.astype(BF16), upto)
    slot = jnp.sum(marks * ranks, axis=0, keepdims=True).astype(I32) - 1
    high = (row // 16).astype(F32)
    low = (row % 16).astype(F32)
    values = jnp.concatenate([marks * high, marks * low], axis=0).astype(BF16)
    places = jnp.where(iota((LANES, tokens), 0) == slot + lane0, 1.0, 0.0).astype(BF16)
    wanted = dot(values, places, NT)
    wanted = wanted[:shards] * 16.0 + wanted[shards:]
    return owner * CAP + slot, wanted.astype(I32)


DURING = {0: [(0, 0)], 1: [(0, 1), (1, 0)], 2: [(1, 1), (2, 0)], 3: [(2, 1), (3, 0)]}


def batches_of(layers):
    return [(l, 1) for l in reversed(range(layers))]


def window_kernel(shards, seq_axis, chunk,
                  owner_ref, row_ref, table_ref, gain_ref, weight_hbm, up_hbm,
                  weight_out, gain_out, table_out,
                  ask, asked, serve, fetched, back, returned, pick, place, add,
                  weight_ref, up_ref, wide, padded, conv, normed, inverse, slope, hidden, dwide, grad_ref,
                  dweight_ref, tsend, trecv, s0, r0, s1, g0, g1, g2, g3,
                  load_sem, send_sem, recv_sem, wsend, wrecv, *work):
    sizes = plan(shards, seq_axis)
    z_size, y_size, _, x_size = sizes
    layers, taps, width = weight_ref.shape
    tokens = row_ref.shape[1]
    rows = table_ref.shape[0]
    slots = shards * CAP
    groups = shards // 8
    e, x = lax.axis_index("emb"), lax.axis_index("seq")
    c = lax.rem(e, 2)
    y = lax.rem(e // 2, y_size)
    z = e // (2 * y_size)
    _, device = emb_peer(shards)
    sibling = (e + 1 - 2 * c, x)
    half = taps // 2
    sets = batches_of(layers)
    count = len(sets)
    r1 = work[:count]
    r3, s2, r2, t2 = (work[count + 2 * k : count + 2 * k + 2] for k in range(4))
    plane = x_size * y_size
    p_me = x * y_size + y
    high = half // (plane // 2)

    def x_index(k):
        return lax.rem(x + k + 1, x_size)

    def x_device(k):
        return (e, x_index(k))

    def y_index(k):
        return lax.rem(y + k + 1, y_size)

    def y_device(k):
        return ((z * y_size + y_index(k)) * 2 + c, x)

    def p_index(k):
        return lax.rem(p_me + k + 1, plane)

    def p_device(k):
        p = p_index(k)
        return ((z * y_size + lax.rem(p, y_size)) * 2 + c, p // y_size)

    def off_device(k):
        py = lax.rem(y + 1 + lax.rem(k, y_size - 1), y_size)
        px = lax.rem(x + 1 + k // (y_size - 1), x_size)
        return ((z * y_size + py) * 2 + c, px)

    def z_index(k):
        return lax.rem(z + k + 1, z_size)

    def z_device(k):
        return ((z_index(k) * y_size + y) * 2 + c, x)

    def remote(src, dst, send, recv, to):
        return pltpu.make_async_remote_copy(
            src_ref=src, dst_ref=dst, send_sem=send, recv_sem=recv, device_id=to, device_id_type=pl.DeviceIdType.MESH
        )

    load_weight = pltpu.make_async_copy(weight_hbm, weight_ref, load_sem.at[0])
    load_up = pltpu.make_async_copy(up_hbm, up_ref, load_sem.at[1])
    load_weight.start()
    load_up.start()
    expected = greet([(shards - 1, device), (x_size - 1, x_device), ((x_size - 1) * (y_size - 1), off_device)])

    lane0 = lax.rem(e, 8) * CAP
    places = []
    for m in range(MB):
        q, wanted = requests(owner_ref[m], row_ref[m : m + 1, :], shards, lane0)
        ask[:, m, :] = wanted
        places.append(q)
    pl.semaphore_wait(pltpu.get_barrier_semaphore(), expected)
    pltpu.make_async_copy(ask.at[e], asked.at[e], recv_sem.at[0]).start()
    to_emb(sizes, lambda peer: ask.at[peer], asked.at[e], send_sem.at[0], recv_sem.at[0])

    for m in range(MB):
        column = jnp.broadcast_to(places[m].astype(F32), (LANES, tokens)).T
        for s in range(0, slots, LANES):
            pick[m, :, s : s + LANES] = jnp.where(
                column == (iota((tokens, LANES), 1) + s).astype(F32), 1.0, 0.0
            ).astype(BF16)
            place[m, s : s + LANES, :] = jnp.where(iota((LANES, tokens), 0) + s == places[m], 1.0, 0.0).astype(BF16)
    load_weight.wait()
    for l in range(layers):
        wide[l] = weight_ref[l].astype(BF16)
    pad = (padded.shape[0] - tokens) // 2
    padded[0:pad, :] = jnp.zeros((pad, width), F32)
    padded[pad + tokens :, :] = jnp.zeros((pad, width), F32)

    here = pl.ds(pl.multiple_of(e * CAP, CAP), CAP)
    whole(asked, recv_sem.at[0])
    wanted = []
    for m in range(MB):
        ids = jnp.sum(asked[:, m, :].reshape(groups, 8, LANES), axis=1)
        wanted.append(ids)
        tall = jnp.concatenate([ids.astype(F32)] * (LANES // groups), axis=0).T
        for g in range(groups):
            hot = jnp.where(iota((LANES, rows), 1).astype(F32) == tall[:, g : g + 1], 1.0, 0.0).astype(BF16)
            serve[m, g * LANES : (g + 1) * LANES, :] = dot(hot, table_ref[...]).astype(BF16)
        if m:
            whole(serve.at[0, pl.ds(0, slots - CAP)], send_sem.at[1])
        pltpu.make_async_copy(serve.at[m, here], fetched.at[m, here], recv_sem.at[1 + m]).start()
        to_emb(
            sizes,
            lambda peer, m=m: serve.at[m, pl.ds(pl.multiple_of(peer * CAP, CAP), CAP)],
            fetched.at[m, here],
            send_sem.at[1 + m],
            recv_sem.at[1 + m],
        )
    for m in range(MB):
        for g in range(groups):
            add[m, :, g * LANES : (g + 1) * LANES] = jnp.where(
                iota((rows, LANES), 0) == wanted[m][g : g + 1, :], 1.0, 0.0
            ).astype(BF16)
    load_up.wait()

    spans = [slice(at, at + chunk) for at in range(0, tokens, chunk)]
    inv_width = 1.0 / width
    k0 = math.sqrt(2.0 / math.pi)

    def forward(m):
        conv[...] = dot(pick[m], fetched[m])
        for l in range(layers):
            d = 2**l
            gain = gain_ref[l : l + 1, :]
            for at in spans:
                if l == 0:
                    state = conv[at, :]
                else:
                    state = normed[m, l, at, :]
                centred = state - jnp.sum(state, axis=-1, keepdims=True) * inv_width
                rstd = lax.rsqrt(jnp.sum(centred * centred, axis=-1, keepdims=True) * inv_width + 1e-05)
                norm = centred * rstd
                if l < layers - 1:
                    normed[m, l + 1, at, :] = state
                normed[m, l, at, :] = norm
                inverse[m, l, at, :] = jnp.broadcast_to(rstd, (chunk, LANES))
                padded[pad + at.start : pad + at.stop, :] = norm * gain
            for k in range(3):
                for at in spans:
                    moved = padded[pad + at.start - k * d : pad + at.stop - k * d, :]
                    hidden[m, l, at, k * width : (k + 1) * width] = moved.astype(BF16)
            conv[...] = dot(hidden[m, l], wide[l])
            for at in spans:
                v = conv[at, :]
                v2 = v * v
                t = jnp.tanh(v * (k0 + (k0 * 0.044715) * v2))
                side = 0.5 + 0.5 * t
                slope[m, l, at, :] = side + v * (0.5 - 0.5 * t * t) * (k0 + (3 * k0 * 0.044715) * v2)
                if l < layers - 1:
                    state = normed[m, l + 1, at, :]
                    normed[m, l + 1, at, :] = (state + v * side).astype(BF16).astype(F32)

    def backward(m, after):
        for l in reversed(range(layers)):
            d = 2**l
            gain = gain_ref[l : l + 1, :]
            src = up_ref if l == layers - 1 else grad_ref
            for at in spans:
                padded[pad + at.start : pad + at.stop, :] = src[m, at, :].astype(F32) * slope[m, l, at, :]
            for k in range(3):
                for at in spans:
                    moved = padded[pad + at.start + k * d : pad + at.stop + k * d, :]
                    dwide[m, at, k * width : (k + 1) * width] = moved.astype(BF16)
            for k in range(3):
                part = dot(hidden[m, l, :, 0:width], dwide[m, :, k * width : (k + 1) * width], TN)
                taken = slice(k * width, (k + 1) * width)
                if m == 0:
                    dweight_ref[l, taken, :] = part
                else:
                    dweight_ref[l, taken, :] += part
            dh = dot(dwide[m, :, 0:width], wide[l, 0:width, :], NT)
            dh = dh + dot(dwide[m, :, width : 2 * width], wide[l, width : 2 * width, :], NT)
            dh = dh + dot(dwide[m, :, 2 * width :], wide[l, 2 * width :, :], NT)
            conv[...] = dh
            dgain = jnp.zeros((1, width), F32)
            for at in spans:
                dh = conv[at, :]
                norm = normed[m, l, at, :]
                both = dh * norm
                dgain = dgain + jnp.sum(both, axis=0, keepdims=True)
                dn = dh * gain
                m1 = jnp.sum(dn, axis=-1, keepdims=True) * inv_width
                m2 = jnp.sum(both * gain, axis=-1, keepdims=True) * inv_width
                rstd = inverse[m, l, at, 0:1]
                grad_ref[m, at, :] = (
                    src[m, at, :].astype(F32) + rstd * (dn - m1 - norm * m2)
                ).astype(BF16)
            if m == 0:
                g0[0, l : l + 1, :] = dgain
            else:
                g0[0, l : l + 1, :] += dgain
            after(l)

    def line_up(m):
        for s in range(0, slots, LANES):
            back[m, s : s + LANES, :] = dot(place[m, s : s + LANES, :], grad_ref[m]).astype(BF16)
        pltpu.make_async_copy(back.at[m, here], returned.at[m, here], recv_sem.at[3 + m]).start()

    def send_back(m, rounds=None):
        to_emb(
            sizes,
            lambda peer: back.at[m, pl.ds(pl.multiple_of(peer * CAP, CAP), CAP)],
            returned.at[m, here],
            send_sem.at[3 + m],
            recv_sem.at[3 + m],
            rounds,
        )

    theirs = pl.ds(pl.multiple_of((1 - c) * half, half), half)
    ours = pl.ds(pl.multiple_of(c * half, half), half)


    def of(b):
        return pl.ds(sets[b][0], sets[b][1])

    def piece(some, p, start):
        return (
            some,
            pl.ds(pl.multiple_of(start + (p // 2) * high, 16), high),
            pl.ds(pl.multiple_of(lax.rem(p, 2) * LANES, LANES), LANES),
        )

    def added(ref, size):
        total = ref[0].astype(F32)
        for k in range(1, size):
            total = total + ref[k].astype(F32)
        return total

    def pair(b):
        for l in range(sets[b][0], sum(sets[b])):
            s0[l] = dweight_ref[l, theirs, :].astype(BF16)
        remote(s0.at[of(b)], r0.at[of(b)], wsend.at[0, b], wrecv.at[0, b], sibling).start()

    def across(b):
        whole(r0.at[of(b)], wrecv.at[0, b])
        for l in range(sets[b][0], sum(sets[b])):
            s1[l] = (dweight_ref[l, ours, :] + r0[l].astype(F32)).astype(BF16)
        pltpu.make_async_copy(s1.at[piece(of(b), p_me, 0)], r1[b].at[p_me], wrecv.at[1, b]).start()
        scatter_to(
            plane - 1, p_device, lambda k: s1.at[piece(of(b), p_index(k), 0)], r1[b].at[p_me], wsend.at[1, b], wrecv.at[1, b]
        )

    deep = layers // 2
    per_z = deep * high // z_size

    def along(h):
        parts = []
        for l in range(h * deep, (h + 1) * deep):
            b = layers - 1 - l
            whole(r1[b], wrecv.at[1, b])
            parts.append(added(r1[b], plane).reshape(high, LANES))
        total = jnp.concatenate(parts, axis=0)
        for k in range(z_size):
            s2[h][k, 0:per_z, :] = total[k * per_z : (k + 1) * per_z].astype(BF16)
        pltpu.make_async_copy(s2[h].at[z], r2[h].at[z], wrecv.at[2, h]).start()
        scatter_to(z_size - 1, z_device, lambda k: s2[h].at[z_index(k)], r2[h].at[z], wsend.at[2, h], wrecv.at[2, h])

    def told(h):
        whole(r2[h], wrecv.at[2, h])
        t2[h][z] = added(r2[h], z_size).astype(BF16)
        scatter_to(z_size - 1, z_device, lambda k: t2[h].at[z], t2[h].at[z], wsend.at[5, h], wrecv.at[5, h])

    def across_back(h):
        whole(t2[h].at[pl.ds(0, z_size - 1)], wrecv.at[5, h])
        total = jnp.concatenate([t2[h][k, 0:per_z, :].astype(F32) for k in range(z_size)], axis=0)
        r3[h][...] = total.reshape(deep, high, LANES).astype(BF16)
        spot = weight_out.at[piece(pl.ds(h * deep, deep), p_me, c * half)]
        pltpu.make_async_copy(r3[h], spot, wrecv.at[3, h]).start()
        scatter_to(plane - 1, p_device, lambda k: r3[h], spot, wsend.at[3, h], wrecv.at[3, h])

    def pair_back(h):
        done = weight_out.at[pl.ds(h * deep, deep), ours]
        whole(done, wrecv.at[3, h])
        remote(done, done, wsend.at[4, h], wrecv.at[4, h], sibling).start()

    way = [pair, across]

    def advance(*steps):
        for b, phase in steps:
            way[phase](b)

    def gain_axis(phase, me, size, to, source, ref):
        ref[me] = source
        scatter_to(size - 1, to, lambda k: ref.at[me], ref.at[me], wsend.at[phase, count], wrecv.at[phase, count])

    def gain_sum(phase, size, ref):
        whole(ref.at[pl.ds(0, size - 1)], wrecv.at[phase, count])
        return added(ref, size)

    def during(l):
        for step in DURING.get(layers - 1 - l, ()):
            advance(step)

    whole(fetched.at[0], recv_sem.at[1])
    forward(0)
    g0[0] = jnp.zeros_like(g0[0])
    backward(0, lambda l: None)
    line_up(0)
    send_back(0)
    whole(fetched.at[1], recv_sem.at[2])
    forward(1)
    backward(1, during)

    gain_pair = remote(g0.at[0], g0.at[1], wsend.at[0, count], wrecv.at[0, count], sibling)
    gain_pair.start()
    line_up(1)
    advance((layers - 1, 1))
    along(1)
    rounds = 2 * y_size
    send_back(1, (0, rounds // 2))
    gain_pair.wait_recv()
    gain_axis(1, x, x_size, x_device, g0[0] + g0[1], g1)
    along(0)
    told(1)
    gain_axis(2, y, y_size, y_device, gain_sum(1, x_size, g1), g2)
    send_back(1, (rounds // 2, rounds * 3 // 4))
    whole(returned.at[0], recv_sem.at[3])
    conv[0:rows, :] = dot(add[0], returned[0])
    told(0)
    send_back(1, (rounds * 3 // 4, rounds))
    gain_axis(3, z, z_size, z_device, gain_sum(2, y_size, g2), g3)
    across_back(1)
    across_back(0)

    share = rows // x_size
    whole(returned.at[1], recv_sem.at[4])
    tsend[...] = (conv[0:rows, :] + dot(add[1], returned[1])).astype(BF16).reshape(x_size, share, width)
    pltpu.make_async_copy(tsend.at[x], trecv.at[x], recv_sem.at[5]).start()
    scatter_to(x_size - 1, x_device, lambda k: tsend.at[x_index(k)], trecv.at[x], send_sem.at[5], recv_sem.at[5])
    pair_back(1)
    whole(trecv, recv_sem.at[5])
    table_out[x] = added(trecv, x_size).astype(BF16)
    scatter_to(x_size - 1, x_device, lambda k: table_out.at[x], table_out.at[x], send_sem.at[6], recv_sem.at[6])

    pair_back(0)
    gain_out[...] = gain_sum(3, z_size, g3)
    for h in range(2):
        whole(weight_out.at[pl.ds(h * deep, deep), theirs], wrecv.at[4, h])
    whole(table_out.at[pl.ds(0, x_size - 1)], recv_sem.at[6])

    whole(ask.at[pl.ds(0, shards - 1)], send_sem.at[0])
    for m in range(MB):
        if m:
            whole(serve.at[m, pl.ds(0, slots - CAP)], send_sem.at[1 + m])
        whole(back.at[m, pl.ds(0, slots - CAP)], send_sem.at[3 + m])
    whole(tsend.at[pl.ds(0, x_size - 1)], send_sem.at[5])
    whole(tsend.at[pl.ds(0, x_size - 1)], send_sem.at[6])
    for b in range(count):
        whole(s0.at[of(b)], wsend.at[0, b])
        whole(r1[b].at[pl.ds(0, plane - 1)], wsend.at[1, b])
    for h in range(2):
        for _ in range(deep):
            whole(r1[0].at[pl.ds(0, plane - 1)], wsend.at[3, h])
        whole(weight_out.at[pl.ds(h * deep, deep), ours], wsend.at[4, h])
        whole(s2[h].at[pl.ds(0, z_size - 1)], wsend.at[2, h])
        whole(t2[h].at[pl.ds(0, z_size - 1)], wsend.at[5, h])
    gain_pair.wait_send()
    whole(g1.at[pl.ds(0, x_size - 1)], wsend.at[1, count])
    whole(g2.at[pl.ds(0, y_size - 1)], wsend.at[2, count])
    whole(g3.at[pl.ds(0, z_size - 1)], wsend.at[3, count])


def scale_kernel(scale, weight_ref, gain_ref, table_ref, weight_out, gain_out, table_out):
    weight_out[...] = weight_ref[...].astype(F32) * scale
    gain_out[...] = gain_ref[...] * scale
    table_out[...] = table_ref[...].astype(F32)


def body(table, owner, row, conv_weight, gain, upstream):
    shards, seq_axis = lax.axis_size("emb"), lax.axis_size("seq")
    _, tokens = row.shape
    rows, width = table.shape
    layers, taps, _ = conv_weight.shape
    slots = shards * CAP
    z_size, y_size, _, x_size = plan(shards, seq_axis)
    sets = batches_of(layers)
    shape = jax.ShapeDtypeStruct
    dma = pltpu.SemaphoreType.DMA
    half = taps // 2
    share = rows // x_size
    plane = x_size * y_size
    high = half // (plane // 2)
    one_z = (z_size, -(-(layers // 2) * high // z_size // 16) * 16, LANES)
    shapes = [(plane, n, high, LANES) for _, n in sets] + [(layers // 2, high, LANES)] * 2 + [one_z] * 6
    work = [pltpu.VMEM(dims, BF16) for dims in shapes]
    near = pl.BlockSpec(memory_space=pltpu.VMEM)
    far = pl.BlockSpec(memory_space=pl.ANY)
    weight_sum, gain_sum, table_grad = pl.pallas_call(
        functools.partial(window_kernel, shards, seq_axis, 64),
        out_shape=[
            shape((layers, taps, width), BF16),
            shape((layers, width), F32),
            shape((x_size, share, width), BF16),
        ],
        in_specs=[near, near, near, near, far, far],
        out_specs=[near, near, near],
        scratch_shapes=[
            pltpu.VMEM((shards, MB, LANES), I32),
            pltpu.VMEM((shards, MB, LANES), I32),
            pltpu.VMEM((MB, slots, width), BF16),
            pltpu.VMEM((MB, slots, width), BF16),
            pltpu.VMEM((MB, slots, width), BF16),
            pltpu.VMEM((MB, slots, width), BF16),
            pltpu.VMEM((MB, tokens, slots), BF16),
            pltpu.VMEM((MB, slots, tokens), BF16),
            pltpu.VMEM((MB, rows, slots), BF16),
            pltpu.VMEM((layers, taps, width), F32),
            pltpu.VMEM((MB, tokens, width), BF16),
            pltpu.VMEM((layers, taps, width), BF16),
            pltpu.VMEM((tokens + 32, width), F32),
            pltpu.VMEM((max(tokens, rows), width), F32),
            pltpu.VMEM((MB, layers, tokens, width), F32),
            pltpu.VMEM((MB, layers, tokens, LANES), F32),
            pltpu.VMEM((MB, layers, tokens, width), F32),
            pltpu.VMEM((MB, layers, tokens, taps), BF16),
            pltpu.VMEM((MB, tokens, taps), BF16),
            pltpu.VMEM((MB, tokens, width), BF16),
            pltpu.VMEM((layers, taps, width), F32),
            pltpu.VMEM((x_size, share, width), BF16),
            pltpu.VMEM((x_size, share, width), BF16),
            pltpu.VMEM((layers, half, width), BF16),
            pltpu.VMEM((layers, half, width), BF16),
            pltpu.VMEM((layers, half, width), BF16),
            pltpu.VMEM((2, layers, width), F32),
            pltpu.VMEM((x_size, layers, width), F32),
            pltpu.VMEM((y_size, layers, width), F32),
            pltpu.VMEM((z_size, layers, width), F32),
            dma((2,)),
            dma((7,)),
            dma((7,)),
            dma((6, len(sets) + 1)),
            dma((6, len(sets) + 1)),
            *work,
        ],
        compiler_params=pltpu.CompilerParams(
            collective_id=0, has_side_effects=True, vmem_limit_bytes=60 * 2**20
        ),
    )(owner.reshape(MB, 1, tokens), row, table, gain, conv_weight, upstream)
    scale = float(MB * tokens * shards * seq_axis) ** (-0.5)
    halves = [
        pl.BlockSpec((layers // 2, taps, width), lambda k: (k, 0, 0)),
        pl.BlockSpec((layers, width), lambda k: (0, 0)),
        pl.BlockSpec((rows // 2, width), lambda k: (k, 0)),
    ]
    return pl.pallas_call(
        functools.partial(scale_kernel, scale),
        grid=(2,),
        out_shape=[shape((layers, taps, width), F32), shape((layers, width), F32), shape((rows, width), F32)],
        in_specs=halves,
        out_specs=halves,
        compiler_params=pltpu.CompilerParams(vmem_limit_bytes=60 * 2**20),
    )(weight_sum, gain_sum, table_grad.reshape(rows, width))


def solution(mesh):
    in_specs = (
        P("emb", None),
        P(("emb", "seq"), None, None),
        P(("emb", "seq"), None),
        P(),
        P(),
        P(("emb", "seq"), None, None),
    )
    out_specs = (P(), P(), P("emb", None))
    return jax.shard_map(body, mesh=mesh, in_specs=in_specs, out_specs=out_specs, check_vma=False)
```
